32 devices in a mesh: dp: 16 (over z, y, x), outer: 2 (over core).
Axes of the slice: x: 2, y: 2, z: 4, core: 2. Of those that a mesh axis runs over, the one named last changes fastest.
Arguments:
- patches: bfloat16 [384, 196, 768], P(('dp', 'outer'))
- image_counts: int32 [32], P(('dp', 'outer')), may hold values from 1 to 12, 288 in all
- grad_out: bfloat16 [384, 196, 768], P(('dp', 'outer')), may hold values from -6 to 6
- ln1_gain: bfloat16 [768], P('dp'), may hold values from 0.25 to 1.75
- ln1_bias: bfloat16 [768], P('dp'), may hold values from -1.5 to 1.5
- w_token_in: bfloat16 [196, 384], P(None, 'dp'), may hold values from -0.4375 to 0.4375
- b_token_in: bfloat16 [384], P('dp'), may hold values from -1.5 to 1.5
- w_token_out: bfloat16 [384, 196], P('dp'), may hold values from -0.625 to 0.625
- b_token_out: bfloat16 [196], replicated, may hold values from -1.5 to 1.5
- ln2_gain: bfloat16 [768], P('dp'), may hold values from 0.25 to 1.75
- ln2_bias: bfloat16 [768], P('dp'), may hold values from -1.5 to 1.5
- w_chan_in: bfloat16 [768, 3072], P('dp'), may hold values from -0.21875 to 0.21875
- b_chan_in: bfloat16 [3072], P('dp'), may hold values from -1.5 to 1.5
- w_chan_out: bfloat16 [3072, 768], P(None, 'dp'), may hold values from -0.21875 to 0.21875
- b_chan_out: bfloat16 [768], P('dp'), may hold values from -1.5 to 1.5
Outputs:
- mixed: bfloat16 [384, 196, 768], P(('dp', 'outer'))
- grad_patches: float32 [384, 196, 768], P(('dp', 'outer'))
- grad_ln1_gain: float32 [768], P('dp')
- grad_ln1_bias: float32 [768], P('dp')
- grad_w_token_in: float32 [196, 384], P(None, 'dp')
- grad_b_token_in: float32 [384], P('dp')
- grad_w_token_out: float32 [384, 196], P('dp')
- grad_b_token_out: float32 [196], replicated
- grad_ln2_gain: float32 [768], P('dp')
- grad_ln2_bias: float32 [768], P('dp')
- grad_w_chan_in: float32 [768, 3072], P('dp')
- grad_b_chan_in: float32 [3072], P('dp')
- grad_w_chan_out: float32 [3072, 768], P(None, 'dp')
- grad_b_chan_out: float32 [768], P('dp')
The draws below stay inside these ranges and needn't reach their ends.
Inputs may be any that keep to these rules, and one draw needn't show every extreme that they name: `image_counts`: entry j counts the live images of device j along dp+outer; they are that device's first slots of its 12, the others are padding. Some device is full in every draw.
All inputs are finite; a program needn't handle non-finite values.
Results may differ from the reference program's by a relative error of at most 0.015.
Values may be sent and summed in bfloat16 or wider, within the bound.
A program may use at most 256 MiB of HBM per device.

```python
import math
import jax
import jax.numpy as jnp
import numpy as np
from jax import lax

D = 768
S = 196
DS = 384
DC = 3072
IMG_DEV = 12
IMAGES = 384
N_DP = 16
N_OUTER = 2


def draw_patches(key, part):
    key = jax.random.fold_in(key, 11)
    key_base, key_rows, key_cols = jax.random.split(key, 3)
    base = jax.random.normal(key_base, (IMAGES, S, D), jnp.float32)
    small_end, large_end = (0.3, 3.0)
    row_scale = jnp.exp(jax.random.uniform(key_rows, (IMAGES, S, 1), jnp.float32, math.log(small_end), math.log(large_end)))
    col_scale = jnp.exp(jax.random.uniform(key_cols, (1, 1, D), jnp.float32, math.log(small_end), math.log(large_end)))
    return (base * row_scale * col_scale).astype(jnp.bfloat16)


def raised(values, key, source, target, shards_of, factor):
    def block_of(position):
        return (jnp.arange(values.shape[position]) // (values.shape[position] // shards_of)).reshape((-1,) + (1,) * (values.ndim - 1 - position))

    near = jax.random.permutation(key, shards_of)[block_of(target)]
    far = (block_of(target) + shards_of // 2) % shards_of
    return jnp.where((block_of(source) == near) | (block_of(source) == far), factor * values, values)


def block_levels(rng, extent, shards, low, top_value):
    def one(position, shards_of):
        heights = jax.random.uniform(jax.random.fold_in(jax.random.fold_in(rng, 6), position), (shards_of,), jnp.float32, low / len(shards), top_value / len(shards))
        return jnp.repeat(jnp.exp(heights), extent[position] // shards_of).reshape((-1,) + (1,) * (len(extent) - position - 1))

    level = one(*shards[0])
    for cut in shards[1:]:
        level = level * one(*cut)
    return level


def length_profile(count, total, most, slope):
    weights = [(1 << 20) // math.isqrt(rank ** slope) + 1 for rank in range(2, count + 1)]
    rest, holding = total - most - (count - 1), [1] * (count - 1)
    while rest > 0:
        candidates = [i for i in range(count - 1) if holding[i] < most]
        mass, left = sum([weights[i] for i in candidates]), rest
        for i in candidates:
            extra = min(most - holding[i], max(1, left * weights[i] // mass), rest)
            holding[i] = holding[i] + extra
            rest = rest - extra
    return np.array([most] + holding)


def ragged_sizes(rng, amount, total, most, skew):
    if amount == 2:
        one = jax.random.randint(rng, (), max(1, total - most), min(most, total - 1) + 1)
        return jnp.stack([one, total - one])
    tallies = jnp.asarray(length_profile(amount, total, most, skew), jnp.int32)
    couples = (amount - 1) // 2
    source_of, sink = tallies[1:1 + 2 * couples:2], tallies[2:2 + 2 * couples:2]
    room = jnp.minimum(source_of - 1, most - sink)
    shifted = jax.random.randint(jax.random.fold_in(rng, 1), (couples,), 0, 1 << 20) % (room + 1)
    tallies = tallies.at[1:1 + 2 * couples:2].set(source_of - shifted).at[2:2 + 2 * couples:2].set(sink + shifted)
    return tallies[jax.random.permutation(jax.random.fold_in(rng, 2), amount)]


def gaussian(own_key, shape, width, most, pieces=(), kind=jnp.bfloat16):
    values = jax.random.normal(own_key, shape, jnp.float32) * width
    if len(pieces) > 0:
        values = block_levels(own_key, shape, pieces, -0.22, 0.18) * values
    return jnp.clip(values, min=-most, max=most).astype(kind)


def bell_draw_with(own_key, extent, deviation, reach, pieces, heavy, held_as=jnp.bfloat16):
    drawn = deviation * jax.random.normal(own_key, extent, jnp.float32)
    if pieces:
        drawn = drawn * block_levels(own_key, extent, pieces, -0.22, 0.18)
    return jnp.clip(raised(drawn, jax.random.fold_in(own_key, 3), *heavy), -reach, reach).astype(held_as)


def setup_inputs(seed: int = 0) -> dict:
    arg_keys = jax.random.split(jax.random.key(seed), 16)
    return {
        "patches": draw_patches(jax.random.fold_in(arg_keys[15], 71), 0),
        "image_counts": ragged_sizes(arg_keys[1], N_DP * N_OUTER, N_DP * N_OUTER * IMG_DEV * 3 // 4, IMG_DEV, 1).astype(jnp.int32),
        "grad_out": bell_draw_with(arg_keys[2], (IMAGES, S, D), 1.0, 6.0, ((0, 32),), (0, 2, 32, 2.75)),
        "ln1_gain": jnp.clip(1.0 + 0.15 * jax.random.normal(arg_keys[3], (D,), jnp.float32), 0.25, 1.75).astype(jnp.bfloat16),
        "ln1_bias": gaussian(arg_keys[4], (D,), 0.3, 1.5, ((0, 16),)),
        "w_token_in": gaussian(arg_keys[5], (S, DS), S ** -0.5, 0.4375, ((1, 16),)),
        "b_token_in": gaussian(arg_keys[6], (DS,), 0.3, 1.5, ((0, 16),)),
        "w_token_out": gaussian(arg_keys[7], (DS, S), (DS // 4) ** -0.5, 0.625, ((0, 16),)),
        "b_token_out": gaussian(arg_keys[8], (S,), 0.3, 1.5),
        "ln2_gain": jnp.clip(1.0 + 0.15 * jax.random.normal(arg_keys[9], (D,), jnp.float32), 0.25, 1.75).astype(jnp.bfloat16),
        "ln2_bias": gaussian(arg_keys[10], (D,), 0.3, 1.5, ((0, 16),)),
        "w_chan_in": gaussian(arg_keys[11], (D, DC), D ** -0.5, 0.21875, ((0, 16),)),
        "b_chan_in": gaussian(arg_keys[12], (DC,), 0.3, 1.5, ((0, 16),)),
        "w_chan_out": gaussian(arg_keys[13], (DC, D), (DC // 4) ** -0.5, 0.21875, ((1, 16),)),
        "b_chan_out": gaussian(arg_keys[14], (D,), 0.3, 1.5, ((0, 16),)),
    }


@jax.custom_vjp
def low(v):
    return lax.optimization_barrier(v.astype(jnp.bfloat16)).astype(jnp.float32)

@jax.custom_vjp
def low_back(v):
    return v

def low_keep(v):
    return (low(v), None)

def low_pass(kept, grad):
    return (grad,)

def back_keep(v):
    return (v, None)

def back_low(kept, grad):
    return (low(grad),)
low.defvjp(low_keep, low_pass)
low_back.defvjp(back_keep, back_low)
eps = 1e-06
batch_images = 16
highest = lax.Precision.HIGHEST

def normalize(values, gain, shift):
    average = lax.optimization_barrier(jnp.mean(values, axis=-1, keepdims=True))
    centered = values - average
    variance = lax.optimization_barrier(jnp.mean(centered * centered, axis=-1, keepdims=True))
    return centered * lax.rsqrt(variance + eps) * gain + shift

def forward(inputs, keep_mask, params):
    gain_one, shift_one, tok_win, tok_bin, tok_wout, tok_bout, gain_two, shift_two, chan_win, chan_bin, chan_wout, chan_bout = params
    token_in = low(normalize(inputs, gain_one, shift_one))
    token_pre = low_back(jnp.einsum('isd,sk->idk', token_in, tok_win, precision=highest) + tok_bin)
    token_act = low(jax.nn.gelu(token_pre, approximate=True))
    token_out = low_back(jnp.einsum('idk,ks->isd', token_act, tok_wout, precision=highest) + tok_bout[:, None])
    residual = inputs + token_out
    chan_in = low(normalize(residual, gain_two, shift_two))
    chan_pre = low_back(jnp.einsum('isd,dk->isk', chan_in, chan_win, precision=highest) + chan_bin)
    chan_act = low(jax.nn.gelu(chan_pre, approximate=True))
    chan_out = low_back(jnp.einsum('isk,kd->isd', chan_act, chan_wout, precision=highest) + chan_bout)
    return keep_mask[:, None, None] * (residual + chan_out)

def reference(patches, image_counts, grad_out, ln1_gain, ln1_bias, w_token_in, b_token_in, w_token_out, b_token_out, ln2_gain, ln2_bias, w_chan_in, b_chan_in, w_chan_out, b_chan_out):
    params = tuple((p.astype(jnp.float32) for p in (ln1_gain, ln1_bias, w_token_in, b_token_in, w_token_out, b_token_out, ln2_gain, ln2_bias, w_chan_in, b_chan_in, w_chan_out, b_chan_out)))
    slot_ids = jnp.arange(IMAGES, dtype=jnp.int32)
    owners = (slot_ids // IMG_DEV).astype(jnp.int32)
    keep_mask = (slot_ids % IMG_DEV < image_counts[owners]).astype(jnp.float32)
    groups = IMAGES // batch_images
    inputs = patches.astype(jnp.float32).reshape(groups, batch_images, S, D)
    masks = keep_mask.reshape(groups, batch_images)
    cotangents = grad_out.astype(jnp.float32).reshape(groups, batch_images, S, D)

    def group_step(totals, group_item):
        group_in, group_mask, group_grad = group_item
        result, pull_back = jax.vjp(lambda values_in, params_in: forward(values_in, group_mask, params_in), group_in, params)
        grad_in, grad_params = pull_back(group_grad)
        totals = jax.tree.map(lambda left, right: left + right, totals, grad_params)
        return (totals, (result.astype(jnp.bfloat16), grad_in))
    zero_grads = tuple((jnp.zeros_like(p) for p in params))
    totals, (results, grads_in) = lax.scan(group_step, zero_grads, (inputs, masks, cotangents))
    mixed = results.reshape(IMAGES, S, D)
    grad_patches = grads_in.reshape(IMAGES, S, D)
    return (mixed, grad_patches, totals[0], totals[1], totals[2], totals[3], totals[4], totals[5], totals[6], totals[7], totals[8], totals[9], totals[10], totals[11])
```

```python
import functools

import jax
import jax.numpy as jnp
from jax import lax
from jax.experimental import pallas as pl
from jax.experimental.pallas import tpu as pltpu
from jax.sharding import PartitionSpec as P

EPS = 1e-06
F32 = jnp.float32
BF16 = jnp.bfloat16
NN = (((1,), (0,)), ((), ()))
NT = (((1,), (1,)), ((), ()))
TN = (((0,), (0,)), ((), ()))
ROOT = 0.7978845608028654
CUBE = 0.044715 * ROOT


def dot(left, right, dims):
    return lax.dot_general(left, right, dims, preferred_element_type=F32)


def gelu_both(value):
    square = value * value
    half = 0.5 + 0.5 * jnp.tanh(value * (ROOT + CUBE * square))
    slope = half + (half - half * half) * (value * (2 * ROOT + 6 * CUBE * square))
    return value * half, slope


def fold(values):
    return jnp.sum(values.reshape(values.shape[0] // 8, 8, values.shape[1]), axis=0)


def lane_mean(values):
    return jnp.mean(values, axis=-1, keepdims=True)


def standardize(values):
    centered = values - lane_mean(values)
    scale = lax.rsqrt(lane_mean(centered * centered) + EPS)
    return centered * scale, scale


def pad_rows(values, rows):
    extra = rows - values.shape[0]
    if extra == 0:
        return values
    return jnp.concatenate([values, jnp.zeros((extra, values.shape[1]), values.dtype)], axis=0)


class Sizes:
    def __init__(self, images, patches, channels, token_hidden, hidden, width, rows):
        self.images, self.patches, self.channels = images, patches, channels
        self.token_hidden, self.hidden, self.width = token_hidden, hidden, width
        self.padded = -(-patches // 8) * 8
        self.flat = images * self.padded
        self.blocks = hidden // width
        self.rows = rows
        self.chunks = self.flat // rows
        self.pairs = images // 2


def layer_kernel(
    sz,
    keep, patches, grad_out, weights,
    gain1, shift1, gain2, shift2, out_bias, tok_in_bias, tok_out_bias,
    tok_in_t, tok_in, tok_out_t, tok_out, chan_in_bias,
    mixed, grad_patches, kept_act, kept_slope, g_weights,
    g_gain1, g_shift1, g_gain2, g_shift2, g_out_bias, g_tok_in_bias, g_tok_out_bias,
    g_tok_in, g_tok_out, g_chan_in_bias,
    x_all, gout_all, chan_in, xhat2, scale2, masked, total_out, total_din,
    act_slot, slope_slot, act_s, dpre_s, w_slot, gw_slot, mixed_slot, gp_slot,
    load_sem, act_sem, w_sem, gw_sem, out_sem,
):
    pad, flat = sz.padded, sz.flat

    def load_copies(i):
        return (
            pltpu.make_async_copy(patches.at[i], x_all.at[i], load_sem.at[0, i]),
            pltpu.make_async_copy(grad_out.at[i], gout_all.at[i], load_sem.at[1, i]),
        )

    def weight_copies(j, slot):
        cols = pl.ds(pl.multiple_of(j * sz.width, sz.width), sz.width)
        return (
            pltpu.make_async_copy(weights.at[0, :, cols], w_slot.at[slot, 0], w_sem.at[slot, 0]),
            pltpu.make_async_copy(weights.at[1, :, cols], w_slot.at[slot, 1], w_sem.at[slot, 1]),
        )

    def grad_copies(j, slot):
        cols = pl.ds(pl.multiple_of(j * sz.width, sz.width), sz.width)
        return (
            pltpu.make_async_copy(gw_slot.at[slot, 0], g_weights.at[0, :, cols], gw_sem.at[slot, 0]),
            pltpu.make_async_copy(gw_slot.at[slot, 1], g_weights.at[1, :, cols], gw_sem.at[slot, 1]),
        )

    def keep_copies(pair, slot, k):
        i = pair * 2 + k
        return (
            pltpu.make_async_copy(act_slot.at[slot, k], kept_act.at[i], act_sem.at[slot, k, 0]),
            pltpu.make_async_copy(slope_slot.at[slot, k], kept_slope.at[i], act_sem.at[slot, k, 1]),
        )

    def back_copies(pair, slot, k):
        i = pair * 2 + k
        return (
            pltpu.make_async_copy(kept_act.at[i], act_slot.at[slot, k], act_sem.at[slot, k, 0]),
            pltpu.make_async_copy(kept_slope.at[i], slope_slot.at[slot, k], act_sem.at[slot, k, 1]),
        )

    def result_copies(pair, slot, k):
        i = pair * 2 + k
        return (
            pltpu.make_async_copy(mixed_slot.at[slot, k], mixed.at[i], out_sem.at[slot, k, 0]),
            pltpu.make_async_copy(gp_slot.at[slot, k], grad_patches.at[i], out_sem.at[slot, k, 1]),
        )

    def start(copies):
        for copy in copies:
            copy.start()

    def wait(copies):
        for copy in copies:
            copy.wait()

    def load_all(i, carry):
        start(load_copies(i))
        return carry

    lax.fori_loop(0, sz.images, load_all, 0)
    start(weight_copies(0, 0))
    for ref in (g_gain1, g_shift1, g_gain2, g_shift2, g_out_bias, g_tok_in_bias, g_tok_out_bias,
                g_tok_in, g_tok_out, g_chan_in_bias):
        ref[...] = jnp.zeros_like(ref)
    total_din[...] = jnp.zeros_like(total_din)

    def token_forward(pair, carry):
        slot = lax.rem(pair, 2)

        @pl.when(pair >= 2)
        def _():
            for k in range(2):
                wait(keep_copies(pair - 2, slot, k))

        residuals = []
        for k in range(2):
            i = pair * 2 + k
            wait(load_copies(i))
            x = pad_rows(x_all[i].astype(F32), pad)
            xhat, _ = standardize(x)
            token_in = (xhat * gain1[...] + shift1[...]).astype(BF16)
            pre = dot(tok_in_t[...], token_in, NN) + tok_in_bias[...]
            act, slope = gelu_both(pre)
            act = act.astype(BF16)
            act_slot[slot, k] = act
            slope_slot[slot, k] = slope.astype(BF16)
            residuals.append(x + dot(tok_out_t[...], act, NN) + tok_out_bias[...])
        both = pl.ds(pl.multiple_of(pair * 2 * pad, 16), 2 * pad)
        residual = jnp.concatenate(residuals, axis=0)
        hat, scale = standardize(residual)
        chan_in[both, :] = (hat * gain2[...] + shift2[...]).astype(BF16)
        xhat2[both, :] = hat.astype(BF16)
        scale2[both, :] = scale
        total_out[both, :] = residual + out_bias[...]
        cotangent = jnp.concatenate(
            [pad_rows(gout_all[pair * 2 + k].astype(F32), pad) * keep[pair * 2 + k] for k in range(2)], axis=0
        )
        masked[both, :] = cotangent.astype(BF16)
        g_out_bias[...] += fold(cotangent)
        for k in range(2):
            start(keep_copies(pair, slot, k))
        return carry

    lax.fori_loop(0, sz.pairs, token_forward, 0)
    for pair in range(max(0, sz.pairs - 2), sz.pairs):
        for k in range(2):
            wait(keep_copies(pair, pair % 2, k))

    def hidden_block(j, carry):
        slot = lax.rem(j, 2)
        wait(weight_copies(j, slot))

        @pl.when(j + 1 < sz.blocks)
        def _():
            start(weight_copies(j + 1, 1 - slot))

        def row_chunk(r, carry):
            rows = pl.ds(pl.multiple_of(r * sz.rows, 16), sz.rows)
            pre = dot(chan_in[rows, :], w_slot[slot, 0], NN) + chan_in_bias[j]
            d_act = dot(masked[rows, :], w_slot[slot, 1], NN)
            act, slope = gelu_both(pre)
            act = act.astype(BF16)
            d_pre = d_act * slope
            g_chan_in_bias[j] += fold(d_pre)
            d_pre = d_pre.astype(BF16)
            act_s[rows, :] = act
            dpre_s[rows, :] = d_pre
            total_out[rows, :] += dot(act, w_slot[slot, 1], NT)
            total_din[rows, :] += dot(d_pre, w_slot[slot, 0], NT)
            return carry

        lax.fori_loop(0, sz.chunks, row_chunk, 0)

        @pl.when(j >= 2)
        def _():
            wait(grad_copies(j - 2, slot))

        gw_slot[slot, 0] = dot(chan_in[...], dpre_s[...], TN)
        gw_slot[slot, 1] = dot(masked[...], act_s[...], TN)
        start(grad_copies(j, slot))
        return carry

    lax.fori_loop(0, sz.blocks, hidden_block, 0)
    for j in range(max(0, sz.blocks - 2), sz.blocks):
        wait(grad_copies(j, j % 2))
    for k in range(2):
        start(back_copies(0, 0, k))

    def token_backward(pair, carry):
        slot = lax.rem(pair, 2)

        @pl.when(pair + 1 < sz.pairs)
        def _():
            for k in range(2):
                start(back_copies(pair + 1, 1 - slot, k))

        @pl.when(pair >= 2)
        def _():
            for k in range(2):
                wait(result_copies(pair - 2, slot, k))

        both = pl.ds(pl.multiple_of(pair * 2 * pad, 16), 2 * pad)
        d_in = total_din[both, :]
        hat = xhat2[both, :].astype(F32)
        g_gain2[...] += fold(d_in * hat)
        g_shift2[...] += fold(d_in)
        e = d_in * gain2[...]
        d_residual = masked[both, :].astype(F32) + scale2[both, :] * (
            e - lane_mean(e) - hat * lane_mean(e * hat)
        )
        d_token_outs = d_residual.astype(BF16)
        rounded = d_token_outs.astype(F32)
        for k in range(2):
            i = pair * 2 + k
            part = slice(k * pad, (k + 1) * pad)
            wait(back_copies(pair, slot, k))
            d_token_out = rounded[part].astype(BF16)
            act = act_slot[slot, k]
            g_tok_out[...] += dot(act, d_token_out, NT)
            g_tok_out_bias[...] += jnp.sum(rounded[part], axis=-1, keepdims=True)
            d_pre = dot(tok_out[...], d_token_out, NN) * slope_slot[slot, k].astype(F32)
            g_tok_in_bias[...] += jnp.sum(d_pre, axis=-1, keepdims=True)
            d_pre = d_pre.astype(BF16)
            x = pad_rows(x_all[i].astype(F32), pad)
            hat1, scale1 = standardize(x)
            token_in = (hat1 * gain1[...] + shift1[...]).astype(BF16)
            g_tok_in[...] += dot(d_pre, token_in, NT)
            d_token_in = dot(tok_in[...], d_pre, NN)
            g_gain1[...] += fold(d_token_in * hat1)
            g_shift1[...] += fold(d_token_in)
            f = d_token_in * gain1[...]
            result = d_residual[part] + scale1 * (f - lane_mean(f) - hat1 * lane_mean(f * hat1))
            gp_slot[slot, k] = result[: sz.patches]
            layer = total_out[pl.ds(pl.multiple_of(i * pad, 8), pad), :] * keep[i]
            mixed_slot[slot, k] = layer[: sz.patches].astype(BF16)
            start(result_copies(pair, slot, k))
        return carry

    lax.fori_loop(0, sz.pairs, token_backward, 0)
    for pair in range(max(0, sz.pairs - 2), sz.pairs):
        for k in range(2):
            wait(result_copies(pair, pair % 2, k))


def run_layer(sz, keep, patches, grad_out, weights, small):
    shape = jax.ShapeDtypeStruct
    any_spec, vmem = pl.BlockSpec(memory_space=pl.ANY), pl.BlockSpec(memory_space=pltpu.VMEM)
    smem = pl.BlockSpec(memory_space=pltpu.SMEM)
    images, patch, pad, ch = sz.images, sz.patches, sz.padded, sz.channels
    row8 = shape((8, ch), F32)
    out_shape = (
        shape((images, patch, ch), BF16), shape((images, patch, ch), F32),
        shape((images, sz.token_hidden, ch), BF16), shape((images, sz.token_hidden, ch), BF16),
        shape((2, ch, sz.hidden), F32),
        row8, row8, row8, row8, row8,
        shape((sz.token_hidden, 1), F32), shape((pad, 1), F32),
        shape((sz.token_hidden, pad), F32), shape((sz.token_hidden, pad), F32),
        shape((sz.blocks, 8, sz.width), F32),
    )
    scratch = [
        pltpu.VMEM((images, patch, ch), BF16), pltpu.VMEM((images, patch, ch), BF16),
        pltpu.VMEM((sz.flat, ch), BF16), pltpu.VMEM((sz.flat, ch), BF16),
        pltpu.VMEM((sz.flat, 1), F32), pltpu.VMEM((sz.flat, ch), BF16),
        pltpu.VMEM((sz.flat, ch), F32), pltpu.VMEM((sz.flat, ch), F32),
        pltpu.VMEM((2, 2, sz.token_hidden, ch), BF16), pltpu.VMEM((2, 2, sz.token_hidden, ch), BF16),
        pltpu.VMEM((sz.flat, sz.width), BF16), pltpu.VMEM((sz.flat, sz.width), BF16),
        pltpu.VMEM((2, 2, ch, sz.width), BF16), pltpu.VMEM((2, 2, ch, sz.width), F32),
        pltpu.VMEM((2, 2, patch, ch), BF16), pltpu.VMEM((2, 2, patch, ch), F32),
        pltpu.SemaphoreType.DMA((2, images)), pltpu.SemaphoreType.DMA((2, 2, 2)),
        pltpu.SemaphoreType.DMA((2, 2)), pltpu.SemaphoreType.DMA((2, 2)),
        pltpu.SemaphoreType.DMA((2, 2, 2)),
    ]
    return pl.pallas_call(
        functools.partial(layer_kernel, sz),
        out_shape=out_shape,
        in_specs=[smem, any_spec, any_spec, any_spec] + [vmem] * 12,
        out_specs=[any_spec] * 5 + [vmem] * 10,
        scratch_shapes=scratch,
        compiler_params=pltpu.CompilerParams(vmem_limit_bytes=63 * 2**20),
    )(keep, patches, grad_out, weights, *small)


def on_device(
    patches, image_counts, grad_out,
    ln1_gain, ln1_bias, w_token_in, b_token_in, w_token_out, b_token_out,
    ln2_gain, ln2_bias, w_chan_in, b_chan_in, w_chan_out, b_chan_out,
):
    images, patch, ch = patches.shape
    token_part, hidden_part = b_token_in.shape[0], b_chan_in.shape[0]
    n_dp = lax.axis_size("dp")
    hidden = w_chan_in.shape[1]
    sz = Sizes(images, patch, ch, token_part * n_dp, hidden, 512, images * (-(-patch // 8) * 8) // 3)
    pad = sz.padded
    keep = (jnp.arange(images, dtype=jnp.int32) < image_counts[0]).astype(F32)

    weights = lax.all_gather(jnp.stack([w_chan_in, w_chan_out.T]), "dp", axis=1, tiled=True)
    tokens = lax.all_gather(jnp.stack([w_token_in.T, w_token_out]), "dp", axis=1, tiled=True)
    tokens = jnp.pad(tokens, ((0, 0), (0, 0), (0, pad - patch)))
    vectors = lax.all_gather(
        jnp.concatenate([ln1_gain, ln1_bias, ln2_gain, ln2_bias, b_chan_out, b_token_in, b_chan_in]), "dp", axis=0
    ).astype(F32)
    part = ch // n_dp
    whole = [vectors[:, k * part : (k + 1) * part].reshape(1, ch) for k in range(5)]
    tok_bias = vectors[:, 5 * part : 5 * part + token_part].reshape(-1, 1)
    chan_bias = vectors[:, 5 * part + token_part :].reshape(sz.blocks, 1, sz.width)
    out_bias = jnp.pad(b_token_out.astype(F32), (0, pad - patch))[:, None]
    small = (
        *whole, tok_bias, out_bias, tokens[0], tokens[0].T, tokens[1].T, tokens[1], chan_bias,
    )
    res = run_layer(sz, keep, patches, grad_out, weights, small)
    mixed, grad_patches, _, _, g_weights = res[:5]
    g_weights = lax.psum_scatter(g_weights.astype(BF16), ("dp",), scatter_dimension=1, tiled=True)
    g_weights = lax.psum(g_weights, "outer").astype(F32)
    g_tokens = jnp.stack([res[12], res[13]])
    g_tokens = lax.psum_scatter(g_tokens, ("dp",), scatter_dimension=1, tiled=True)
    g_tokens = lax.psum(g_tokens, "outer")[:, :, :patch]
    g_vec = lax.psum(
        tuple(jnp.sum(v, axis=0) for v in res[5:10])
        + (res[10][:, 0], res[11][:patch, 0], jnp.sum(res[14], axis=1).reshape(-1)),
        ("dp", "outer"),
    )

    def own(vector, length):
        return lax.dynamic_slice_in_dim(vector, lax.axis_index("dp") * length, length)

    return (
        mixed, grad_patches,
        own(g_vec[0], part), own(g_vec[1], part), g_tokens[0].T, own(g_vec[5], token_part), g_tokens[1], g_vec[6],
        own(g_vec[2], part), own(g_vec[3], part), g_weights[0], own(g_vec[7], hidden_part), g_weights[1].T,
        own(g_vec[4], part),
    )


def solution(mesh):
    slots = P(("dp", "outer"), None, None)
    return jax.shard_map(
        on_device,
        mesh=mesh,
        in_specs=(
            slots, P(("dp", "outer")), slots, P("dp"), P("dp"), P(None, "dp"), P("dp"), P("dp", None), P(),
            P("dp"), P("dp"), P("dp", None), P("dp"), P(None, "dp"), P("dp"),
        ),
        out_specs=(
            slots, slots, P("dp"), P("dp"), P(None, "dp"), P("dp"), P("dp", None), P(),
            P("dp"), P("dp"), P("dp", None), P("dp"), P(None, "dp"), P("dp"),
        ),
        check_vma=False,
    )
```

```python
import functools

import jax
import jax.numpy as jnp
from jax import lax
from jax.experimental import pallas as pl
from jax.experimental.pallas import tpu as pltpu
from jax.sharding import PartitionSpec as P

EPS = 1e-06
F32 = jnp.float32
BF16 = jnp.bfloat16
NN = (((1,), (0,)), ((), ()))
NT = (((1,), (1,)), ((), ()))
TN = (((0,), (0,)), ((), ()))
MESH = pl.DeviceIdType.MESH
ROOT = 0.7978845608028654
CUBE = 0.044715 * ROOT


def dot(left, right, dims):
    return lax.dot_general(left, right, dims, preferred_element_type=F32)


def gelu_both(value):
    square = value * value
    half = 0.5 + 0.5 * jnp.tanh(value * (ROOT + CUBE * square))
    slope = half + (half - half * half) * (value * (2 * ROOT + 6 * CUBE * square))
    return value * half, slope


def fold(values):
    return jnp.sum(values.reshape(values.shape[0] // 8, 8, values.shape[1]), axis=0)


def lane_mean(values):
    return jnp.mean(values, axis=-1, keepdims=True)


def standardize(values):
    centered = values - lane_mean(values)
    scale = lax.rsqrt(lane_mean(centered * centered) + EPS)
    return centered * scale, scale


def pad_rows(values, rows):
    extra = rows - values.shape[0]
    if extra == 0:
        return values
    return jnp.concatenate([values, jnp.zeros((extra, values.shape[1]), values.dtype)], axis=0)


class Sizes:
    def __init__(self, images, patches, channels, token_hidden, hidden, width, rows):
        self.images, self.patches, self.channels = images, patches, channels
        self.token_hidden, self.hidden, self.width = token_hidden, hidden, width
        self.padded = -(-patches // 8) * 8
        self.flat = images * self.padded
        self.blocks = hidden // width
        self.rows = rows
        self.chunks = self.flat // rows
        self.pairs = images // 2
        self.lanes = -(-self.padded // 128) * 128


def start(copies):
    for copy in copies:
        copy.start()


def wait(copies):
    for copy in copies:
        copy.wait()


class Place:
    def __init__(self):
        me, c = lax.axis_index("dp"), lax.axis_index("outer")
        z = me // 4
        yx = me - 4 * z
        y = yx // 2
        x = yx - 2 * y
        step_x, step_y = 1 - 2 * x, 2 * (1 - 2 * y)
        self.c, self.z, self.yx = c, z, yx
        self.yx_a = yx + (1 - c) * step_x + c * step_y
        self.yx_b = yx + c * step_x + (1 - c) * step_y
        self.yx_ab = yx + step_x + step_y
        self.sibling = (me, 1 - c)
        self.peer_a, self.peer_b = (4 * z + self.yx_a, c), (4 * z + self.yx_b, c)
        self.z_of = [lax.rem(z + k, 4) for k in range(4)]
        self.peer_z = [(4 * self.z_of[k] + yx, c) for k in range(4)]

    def greet(self):
        barrier = pltpu.get_barrier_semaphore()
        peers = [self.sibling, self.peer_a, self.peer_b] + self.peer_z[1:]
        for peer in peers:
            pl.semaphore_signal(barrier, inc=1, device_id=peer, device_id_type=MESH)
        pl.semaphore_wait(barrier, len(peers))


def remote(source, target, sems, index, peer):
    return pltpu.make_async_remote_copy(
        src_ref=source, dst_ref=target, send_sem=sems[0].at[index], recv_sem=sems[1].at[index],
        device_id=peer, device_id_type=MESH,
    )


class Gather:
    def __init__(self, place, own, view, sems, base):
        self.place, self.own, self.view, self.sems, self.base = place, own, view, sems, base

    def send(self, position, index, peer):
        ref = self.view(self.place.c, slice(None), position)
        return remote(ref, ref, self.sems, self.base + index, peer)

    @property
    def along_z(self):
        place = self.place
        target = self.view(place.c, place.z, place.yx)
        return [remote(self.own, target, self.sems, self.base + k - 1, place.peer_z[k]) for k in (1, 2, 3)]

    @property
    def along_a(self):
        return [self.send(self.place.yx, 3, self.place.peer_a)]

    @property
    def along_b(self):
        place = self.place
        return [self.send(place.yx, 4, place.peer_b), self.send(place.yx_a, 5, place.peer_b)]

    @property
    def swap(self):
        return [self.send(slice(None), 6, self.place.sibling)]

    def to_a(self):
        wait(self.along_z)
        start(self.along_a)

    def to_b(self):
        wait(self.along_a)
        start(self.along_b)

    def to_sibling(self):
        wait(self.along_b)
        start(self.swap)


class Reduce:
    def __init__(self, place, refs, own_out, sems, base, slot):
        (self.mine, csend, crecv, self.send1, self.keep1, recv1, self.send2, self.keep2, recv2,
         self.send3, self.keep3, recv3) = refs
        self.place, self.own_out, self.csend, self.sems, self.base = place, own_out, csend, sems, base
        self.crecv, self.recv1, self.recv2, self.recv3 = crecv.at[slot], recv1.at[slot], recv2.at[slot], recv3.at[slot]

    def send(self, source, target, index, peer):
        return remote(source, target, self.sems, self.base + index, peer)

    @property
    def swap(self):
        return [self.send(self.csend, self.crecv, 0, self.place.sibling)]

    @property
    def along_b(self):
        return [self.send(self.send1, self.recv1, 1, self.place.peer_b)]

    @property
    def along_a(self):
        return [self.send(self.send2, self.recv2, 2, self.place.peer_a)]

    @property
    def along_z(self):
        place = self.place
        return [
            self.send(self.send3.at[place.z_of[k]], self.recv3.at[k - 1], 2 + k, place.peer_z[k]) for k in (1, 2, 3)
        ]

    @property
    def finish(self):
        return [self.send(self.own_out, self.own_out, 6, self.place.sibling)]

    def to_b(self):
        wait(self.swap)
        place = self.place

        def step(z, carry):
            for q, (kept, sent) in enumerate(((place.yx, place.yx_b), (place.yx_a, place.yx_ab))):
                self.keep1[z, q] = self.mine[z, kept] + self.crecv[z, kept].astype(F32)
                self.send1[z, q] = (self.mine[z, sent] + self.crecv[z, sent].astype(F32)).astype(BF16)
            return carry

        lax.fori_loop(0, 4, step, 0)
        start(self.along_b)

    def to_a(self):
        wait(self.along_b)

        def step(z, carry):
            self.keep2[z] = self.keep1[z, 0] + self.recv1[z, 0].astype(F32)
            self.send2[z] = (self.keep1[z, 1] + self.recv1[z, 1].astype(F32)).astype(BF16)
            return carry

        lax.fori_loop(0, 4, step, 0)
        start(self.along_a)

    def to_z(self):
        wait(self.along_a)

        def step(z, carry):
            self.send3[z] = (self.keep2[z] + self.recv2[z].astype(F32)).astype(BF16)
            return carry

        lax.fori_loop(0, 4, step, 0)
        z = self.place.z
        self.keep3[...] = self.keep2[z] + self.recv2[z].astype(F32)
        start(self.along_z)

    def to_owner(self):
        wait(self.along_z)
        total = self.keep3[...]
        for k in range(3):
            total += self.recv3[k].astype(F32)
        self.own_out[...] = total
        start(self.finish)


def reduce_scratch(part, width, slots):
    return [
        pltpu.VMEM((4, 4, part, width), F32),
        pltpu.VMEM((4, 4, part, width), BF16), pltpu.VMEM((slots, 4, 4, part, width), BF16),
        pltpu.VMEM((4, 2, part, width), BF16), pltpu.VMEM((4, 2, part, width), F32),
        pltpu.VMEM((slots, 4, 2, part, width), BF16),
        pltpu.VMEM((4, part, width), BF16), pltpu.VMEM((4, part, width), F32),
        pltpu.VMEM((slots, 4, part, width), BF16),
        pltpu.VMEM((4, part, width), BF16), pltpu.VMEM((part, width), F32),
        pltpu.VMEM((slots, 3, part, width), BF16),
    ]


class Layer:
    def __init__(self, sz, **refs):
        self.sz = sz
        self.__dict__.update(refs)

    def load_copies(self, pair, k):
        i = pair * 2 + k
        return [pltpu.make_async_copy(self.patches.at[i], self.x_all.at[i], self.load_sem.at[i])]

    def cotangent_copies(self, pair, slot):
        return [
            pltpu.make_async_copy(self.grad_out.at[pair * 2 + k], self.mixed_slot.at[slot, k], self.out_sem.at[slot, k, 0])
            for k in range(2)
        ]

    def keep_copies(self, pair, slot, k):
        i = pair * 2 + k
        return [
            pltpu.make_async_copy(self.act_slot.at[slot, k], self.kept_act.at[i], self.act_sem.at[slot, k, 0]),
            pltpu.make_async_copy(self.slope_slot.at[slot, k], self.kept_slope.at[i], self.act_sem.at[slot, k, 1]),
        ]

    def back_copies(self, pair, slot):
        copies = []
        for k in range(2):
            i = pair * 2 + k
            copies += [
                pltpu.make_async_copy(self.kept_act.at[i], self.act_slot.at[slot, k], self.act_sem.at[slot, k, 0]),
                pltpu.make_async_copy(self.kept_slope.at[i], self.slope_slot.at[slot, k], self.act_sem.at[slot, k, 1]),
            ]
        return copies

    def result_copies(self, pair, slot, k):
        i = pair * 2 + k
        return [
            pltpu.make_async_copy(self.mixed_slot.at[slot, k], self.mixed.at[i], self.out_sem.at[slot, k, 0]),
            pltpu.make_async_copy(self.gp_slot.at[slot, k], self.grad_patches.at[i], self.out_sem.at[slot, k, 1]),
        ]

    def begin(self):
        def load_all(pair, carry):
            for k in range(2):
                start(self.load_copies(pair, k))
            return carry

        lax.fori_loop(0, self.sz.pairs, load_all, 0)
        start(self.cotangent_copies(0, 0))

    def clear(self):
        for ref in (self.g_gain1, self.g_shift1, self.g_gain2, self.g_shift2, self.g_out_bias, self.g_tok_out_bias,
                    self.g_tok, self.g_chan_in_bias):
            ref[...] = jnp.zeros_like(ref)

    def both(self, pair):
        return pl.ds(pl.multiple_of(pair * 2 * self.sz.padded, 16), 2 * self.sz.padded)

    def image(self, i):
        return pl.ds(pl.multiple_of(i * self.sz.padded, 8), self.sz.padded)

    def mask_pair(self, pair, carry):
        sz, slot = self.sz, lax.rem(pair, 2)

        @pl.when(pair + 1 < sz.pairs)
        def _():
            start(self.cotangent_copies(pair + 1, 1 - slot))

        wait(self.cotangent_copies(pair, slot))
        cotangent = jnp.concatenate(
            [pad_rows(self.mixed_slot[slot, k].astype(F32), sz.padded) * self.keep[pair * 2 + k] for k in range(2)],
            axis=0,
        )
        self.lhs[1, self.both(pair), :] = cotangent.astype(BF16)
        self.g_out_bias[...] += fold(cotangent)
        return carry

    def norm_pair(self, pair, carry):
        for k in range(2):
            wait(self.load_copies(pair, k))
            i = pair * 2 + k
            xhat, _ = standardize(pad_rows(self.x_all[i].astype(F32), self.sz.padded))
            self.total_din[self.image(i), :] = xhat
        return carry

    def token_input(self, xhat):
        sz = self.sz
        value = xhat * self.gain1[...] + self.shift1[...]
        row = lax.broadcasted_iota(jnp.int32, value.shape, 0)
        return jnp.where(row < sz.patches, value, jnp.where(row == sz.patches, 1.0, 0.0)).astype(BF16)

    def token_forward(self, pair):
        sz, slot = self.sz, lax.rem(pair, 2)

        @pl.when(pair >= 2)
        def _():
            for k in range(2):
                wait(self.keep_copies(pair - 2, slot, k))

        both = self.both(pair)
        residuals = []
        for k in range(2):
            i = pair * 2 + k
            token_in = self.token_input(self.total_din[self.image(i), :])
            act, slope = gelu_both(dot(self.tok_in_t[...], token_in, NN))
            act = act.astype(BF16)
            self.act_slot[slot, k] = act
            self.slope_slot[slot, k] = slope.astype(BF16)
            x = pad_rows(self.x_all[i].astype(F32), sz.padded)
            residuals.append(x + dot(self.tok_out_t[...], act, NN) + self.tok_out_bias[...])
        residual = jnp.concatenate(residuals, axis=0)
        hat, scale = standardize(residual)
        self.lhs[0, both, :] = (hat * self.gain2[...] + self.shift2[...]).astype(BF16)
        self.xhat2[both, :] = hat.astype(BF16)
        self.scale2[both, :] = scale
        self.total_out[both, :] = residual + self.out_bias[...]
        self.total_din[both, :] = jnp.zeros((2 * sz.padded, sz.channels), F32)
        for k in range(2):
            start(self.keep_copies(pair, slot, k))

    def token_forward_end(self):
        for pair in range(max(0, self.sz.pairs - 2), self.sz.pairs):
            for k in range(2):
                wait(self.keep_copies(pair, pair % 2, k))

    def row_chunk(self, j, slot, r):
        sz = self.sz
        rows = pl.ds(pl.multiple_of(r * sz.rows, 16), sz.rows)
        w_in = self.w_slot[slot, 0].reshape(sz.channels, sz.width)
        w_out = self.w_slot[slot, 1].reshape(sz.channels, sz.width)
        pre = dot(self.lhs[0, rows, :], w_in, NN) + self.chan_in_bias[j]
        d_act = dot(self.lhs[1, rows, :], w_out, NN)
        act, slope = gelu_both(pre)
        act = act.astype(BF16)
        d_pre = d_act * slope
        self.g_chan_in_bias[j] += fold(d_pre)
        d_pre = d_pre.astype(BF16)
        self.rhs[1, rows, :] = act
        self.rhs[0, rows, :] = d_pre
        self.total_out[rows, :] += dot(act, w_out, NT)
        self.total_din[rows, :] += dot(d_pre, w_in, NT)

    def weight_grad(self, matrix):
        return dot(self.lhs[matrix], self.rhs[matrix], TN)

    def token_backward(self, pair):
        sz, slot = self.sz, lax.rem(pair, 2)
        pad = sz.padded

        @pl.when(pair + 1 < sz.pairs)
        def _():
            start(self.back_copies(pair + 1, 1 - slot))

        @pl.when(pair >= 2)
        def _():
            for k in range(2):
                wait(self.result_copies(pair - 2, slot, k))

        both = self.both(pair)
        d_in = self.total_din[both, :]
        hat = self.xhat2[both, :].astype(F32)
        self.g_gain2[...] += fold(d_in * hat)
        self.g_shift2[...] += fold(d_in)
        e = d_in * self.gain2[...]
        d_residual = self.lhs[1, both, :].astype(F32) + self.scale2[both, :] * (
            e - lane_mean(e) - hat * lane_mean(e * hat)
        )
        rounded = d_residual.astype(BF16).astype(F32)
        wait(self.back_copies(pair, slot))
        for k in range(2):
            i = pair * 2 + k
            part = slice(k * pad, (k + 1) * pad)
            d_token_out = rounded[part].astype(BF16)
            self.g_tok[1] += dot(self.act_slot[slot, k], d_token_out, NT)
            self.g_tok_out_bias[...] += jnp.sum(rounded[part], axis=-1, keepdims=True)
            d_pre = dot(self.tok_out[...], d_token_out, NN) * self.slope_slot[slot, k].astype(F32)
            d_pre = d_pre.astype(BF16)
            hat1, scale1 = standardize(pad_rows(self.x_all[i].astype(F32), pad))
            self.g_tok[0] += dot(d_pre, self.token_input(hat1), NT)
            d_token_in = dot(self.tok_in[...], d_pre, NN)
            self.g_gain1[...] += fold(d_token_in * hat1)
            self.g_shift1[...] += fold(d_token_in)
            f = d_token_in * self.gain1[...]
            result = d_residual[part] + scale1 * (f - lane_mean(f) - hat1 * lane_mean(f * hat1))
            self.gp_slot[slot, k] = result[: sz.patches]
            layer = self.total_out[self.image(i), :] * self.keep[i]
            self.mixed_slot[slot, k] = layer[: sz.patches].astype(BF16)
            start(self.result_copies(pair, slot, k))

    def token_backward_end(self):
        for pair in range(max(0, self.sz.pairs - 2), self.sz.pairs):
            for k in range(2):
                wait(self.result_copies(pair, pair % 2, k))


def layer_scratch(sz, weight_shape):
    images, patch, ch = sz.images, sz.patches, sz.channels
    return dict(
        x_all=pltpu.VMEM((images, patch, ch), BF16),
        lhs=pltpu.VMEM((2, sz.flat, ch), BF16), xhat2=pltpu.VMEM((sz.flat, ch), BF16),
        scale2=pltpu.VMEM((sz.flat, 1), F32),
        total_out=pltpu.VMEM((sz.flat, ch), F32), total_din=pltpu.VMEM((sz.flat, ch), F32),
        act_slot=pltpu.VMEM((2, 2, sz.token_hidden, ch), BF16),
        slope_slot=pltpu.VMEM((2, 2, sz.token_hidden, ch), BF16),
        rhs=pltpu.VMEM((2, sz.flat, sz.width), BF16),
        w_slot=pltpu.VMEM((2, 2) + weight_shape + (sz.width,), BF16),
        mixed_slot=pltpu.VMEM((2, 2, patch, ch), BF16), gp_slot=pltpu.VMEM((2, 2, patch, ch), F32),
        load_sem=pltpu.SemaphoreType.DMA((images,)), act_sem=pltpu.SemaphoreType.DMA((2, 2, 2)),
        w_sem=pltpu.SemaphoreType.DMA((2, 2)), out_sem=pltpu.SemaphoreType.DMA((2, 2, 2)),
    )


def layer_sums(sz):
    ch = sz.channels
    return dict(
        g_gain1=((8, ch), F32), g_shift1=((8, ch), F32), g_gain2=((8, ch), F32), g_shift2=((8, ch), F32),
        g_out_bias=((8, ch), F32), g_tok_out_bias=((sz.padded, 1), F32),
        g_tok=((2, sz.token_hidden, sz.padded), F32), g_chan_in_bias=((sz.blocks, 8, sz.width), F32),
    )


def layer_params(sz):
    ch, pad, th = sz.channels, sz.padded, sz.token_hidden
    return dict(
        gain1=((1, ch), F32), shift1=((1, ch), F32), gain2=((1, ch), F32), shift2=((1, ch), F32),
        out_bias=((1, ch), F32), tok_in_t=((th, pad), BF16), tok_in=((pad, th), BF16),
        tok_out_t=((pad, th), BF16), tok_out=((th, pad), BF16), chan_in_bias=((sz.blocks, 1, sz.width), F32),
    )


def layer_results(sz):
    return dict(
        mixed=((sz.images, sz.patches, sz.channels), BF16),
        grad_patches=((sz.images, sz.patches, sz.channels), F32),
        kept_act=((sz.images, sz.token_hidden, sz.channels), BF16),
        kept_slope=((sz.images, sz.token_hidden, sz.channels), BF16),
    )


def call_kernel(kernel, inputs, outputs, scratch, **params):
    names = list(inputs) + list(outputs) + list(scratch)

    def body(*refs):
        kernel(dict(zip(names, refs)))

    results = pl.pallas_call(
        body,
        out_shape=[jax.ShapeDtypeStruct(*of) for of, _ in outputs.values()],
        in_specs=[spec for _, spec in inputs.values()],
        out_specs=[spec for _, spec in outputs.values()],
        scratch_shapes=list(scratch.values()),
        compiler_params=pltpu.CompilerParams(vmem_limit_bytes=63 * 2**20, **params),
    )(*[array for array, _ in inputs.values()])
    return dict(zip(outputs, results))


ANYWHERE = pl.BlockSpec(memory_space=pl.ANY)
VMEM = pl.BlockSpec(memory_space=pltpu.VMEM)
SMEM = pl.BlockSpec(memory_space=pltpu.SMEM)


def networked(sz, keep, patches, grad_out, own_weight, own_pack, tok_out_bias):
    part = sz.channels // 16
    tok_part = sz.token_hidden // 16
    pack_rows = own_pack.shape[0]
    blocks, width = sz.blocks, sz.width
    n_gather, n_reduce = blocks + 1, blocks + 1

    def kernel(refs):
        place = Place()
        layer = Layer(sz, **refs)
        gathered, pack_all = refs["gathered"], refs["pack_all"]
        gather_sems = (refs["gather_send"], refs["gather_recv"])
        reduce_sems = (refs["reduce_send"], refs["reduce_recv"])
        vector_sems = (refs["vector_send"], refs["vector_recv"])
        own_out, tok_fin = refs["own_out"], refs["tok_fin"]
        c = place.c
        chan_refs = [refs["chan_net_%d" % k] for k in range(12)]
        tok_refs = [refs["tok_net_%d" % k] for k in range(12)]

        def columns(j):
            return pl.ds(pl.multiple_of(j * width, width), width)

        def gather(j):
            cols = columns(j)

            def view(matrix, z, yx):
                return gathered.at[matrix, z, yx, :, cols]

            return Gather(place, refs["own_weight"].at[:, cols], view, gather_sems, j * 7)

        def pack_view(matrix, z, yx):
            return pack_all.at[matrix, z, yx]

        pack = Gather(place, refs["own_pack"], pack_view, gather_sems, blocks * 7)

        def reduce(j):
            return Reduce(place, chan_refs, own_out.at[c, :, columns(j)], reduce_sems, j * 7, lax.rem(j, 2))

        tok_reduce = Reduce(place, tok_refs, tok_fin.at[c], reduce_sems, blocks * 7, 0)
        own_copies = [
            pltpu.make_async_copy(refs["own_weight"], gathered.at[c, place.z, place.yx], refs["own_sem"].at[0]),
            pltpu.make_async_copy(refs["own_pack"], pack_all.at[c, place.z, place.yx], refs["own_sem"].at[1]),
        ]

        def weight_loads(j, slot):
            return [
                pltpu.make_async_copy(
                    gathered.at[m, :, :, :, columns(j)], layer.w_slot.at[slot, m], layer.w_sem.at[slot, m]
                )
                for m in range(2)
            ]

        start(own_copies)
        layer.begin()
        place.greet()
        start(pack.along_z)
        start(gather(0).along_z)
        layer.clear()
        lax.fori_loop(0, 2, layer.mask_pair, 0)
        wait(own_copies)
        pack.to_a()
        lax.fori_loop(2, sz.pairs, layer.mask_pair, 0)
        pack.to_b()
        gather(0).to_a()
        lax.fori_loop(0, sz.pairs // 2, layer.norm_pair, 0)
        pack.to_sibling()
        lax.fori_loop(sz.pairs // 2, sz.pairs, layer.norm_pair, 0)
        wait(pack.swap)
        start(gather(1).along_z)
        unpack(sz, layer, pack_all, tok_part)

        def forward_step(pair, carry):
            layer.token_forward(pair)

            @pl.when(pair == 0)
            def _():
                gather(0).to_b()
                gather(1).to_a()

            @pl.when(pair == 1)
            def _():
                start(gather(2).along_z)

            @pl.when(pair == 2)
            def _():
                gather(0).to_sibling()
                gather(1).to_b()

            @pl.when(pair == 3)
            def _():
                gather(2).to_a()
                start(gather(3).along_z)

            @pl.when(pair == 4)
            def _():
                wait(gather(0).swap)
                start(weight_loads(0, 0))
                gather(1).to_sibling()

            @pl.when(pair == 5)
            def _():
                gather(2).to_b()
                gather(3).to_a()
                start(gather(4).along_z)

            return carry

        lax.fori_loop(0, sz.pairs, forward_step, 0)
        layer.token_forward_end()

        def block_step(j, carry):
            slot = lax.rem(j, 2)
            wait(weight_loads(j, slot))

            def chunk(r, carry):
                layer.row_chunk(j, slot, r)

                @pl.when(r == 0)
                def _():
                    @pl.when(j >= 1)
                    def _():
                        reduce(j - 1).to_b()

                    @pl.when(j >= 2)
                    def _():
                        reduce(j - 2).to_z()

                @pl.when(r == 1)
                def _():
                    @pl.when(j + 1 < blocks)
                    def _():
                        wait(gather(j + 1).swap)
                        start(weight_loads(j + 1, 1 - slot))

                    @pl.when(j + 2 < blocks)
                    def _():
                        gather(j + 2).to_sibling()

                    @pl.when(j + 3 < blocks)
                    def _():
                        gather(j + 3).to_b()

                    @pl.when(j + 4 < blocks)
                    def _():
                        gather(j + 4).to_a()

                    @pl.when(j + 5 < blocks)
                    def _():
                        start(gather(j + 5).along_z)

                @pl.when(r == 2)
                def _():
                    @pl.when(j >= 1)
                    def _():
                        reduce(j - 1).to_a()

                    @pl.when(j >= 2)
                    def _():
                        reduce(j - 2).to_owner()

                return carry

            lax.fori_loop(0, sz.chunks, chunk, 0)
            mine, csend = chan_refs[0], chan_refs[1]
            csend[...] = layer.weight_grad(1 - c).astype(BF16).reshape(csend.shape)
            start(reduce(j).swap)
            mine[...] = layer.weight_grad(c).reshape(mine.shape)
            return carry

        lax.fori_loop(0, blocks, block_step, 0)
        start(layer.back_copies(0, 0))

        def backward_step(pair, carry):
            layer.token_backward(pair)

            @pl.when(pair == 0)
            def _():
                reduce(blocks - 1).to_b()
                reduce(blocks - 2).to_z()

            @pl.when(pair == 2)
            def _():
                reduce(blocks - 1).to_a()
                reduce(blocks - 2).to_owner()

            @pl.when(pair == 4)
            def _():
                reduce(blocks - 1).to_z()

            return carry

        lax.fori_loop(0, sz.pairs, backward_step, 0)

        mine, csend = tok_refs[0], tok_refs[1]

        def packed(matrix):
            value = layer.g_tok[matrix].reshape(16, tok_part, sz.padded)
            return value

        rows = pl.ds(0, tok_part)
        filler = jnp.zeros((16, pack_rows - tok_part, sz.padded), F32)
        for ref, matrix in ((csend, 1 - c), (mine, c)):
            value = jnp.concatenate([packed(matrix), filler], axis=1).astype(ref.dtype)
            ref[:, :, :, 0 : sz.padded] = value.reshape(4, 4, pack_rows, sz.padded)
            ref[:, :, :, sz.padded :] = jnp.zeros((4, 4, pack_rows, sz.lanes - sz.padded), ref.dtype)
            if ref is csend:
                start(tok_reduce.swap)
        vec, vec_in, vec_z = refs["vec"], refs["vec_in"], refs["vec_z"]
        vec[...] = jnp.zeros_like(vec)
        for k, ref in enumerate((layer.g_gain1, layer.g_shift1, layer.g_gain2, layer.g_shift2, layer.g_out_bias)):
            vec[k : k + 1, :] = jnp.sum(ref[...], axis=0, keepdims=True)
        for j in range(blocks):
            vec[5 + j : 6 + j, 0:width] = jnp.sum(layer.g_chan_in_bias[j], axis=0, keepdims=True)
        column = jnp.broadcast_to(layer.g_tok_out_bias[...], (sz.padded, 128))
        vec[5 + blocks : 6 + blocks, 0 : sz.padded] = jnp.transpose(column)[0:1]

        def vector_swap(k, peer):
            return [remote(vec, vec_in.at[k], vector_sems, k, peer)]

        swaps = [vector_swap(0, place.sibling), vector_swap(1, place.peer_a), vector_swap(2, place.peer_b)]
        vector_z = [remote(vec, vec_z.at[place.z], vector_sems, 2 + k, place.peer_z[k]) for k in (1, 2, 3)]

        def vector_add(k):
            wait(swaps[k])
            vec[...] += vec_in[k]

        start(swaps[0])
        reduce(blocks - 1).to_owner()
        vector_add(0)
        start(swaps[1])
        tok_reduce.to_b()
        vector_add(1)
        start(swaps[2])
        tok_reduce.to_a()
        vector_add(2)
        start(vector_z)
        vec_z[place.z] = vec[...]
        tok_reduce.to_z()
        layer.token_backward_end()
        wait(vector_z)
        refs["vec_out"][...] = (vec_z[0] + vec_z[1]) + (vec_z[2] + vec_z[3])
        tok_reduce.to_owner()

        def finish(j, carry):
            wait(reduce(j).finish)
            return carry

        lax.fori_loop(0, blocks, finish, 0)
        wait(tok_reduce.finish)

    inputs = dict(
        keep=(keep, SMEM), patches=(patches, ANYWHERE), grad_out=(grad_out, ANYWHERE),
        own_weight=(own_weight, ANYWHERE), own_pack=(own_pack, VMEM), tok_out_bias=(tok_out_bias, VMEM),
    )
    outputs = {name: (of, ANYWHERE) for name, of in layer_results(sz).items()}
    outputs["gathered"] = (((2, 4, 4, part, sz.hidden), BF16), ANYWHERE)
    outputs["own_out"] = (((2, part, sz.hidden), F32), VMEM)
    outputs["tok_fin"] = (((2, pack_rows, sz.lanes), F32), VMEM)
    outputs["vec_out"] = (((16, sz.channels), F32), VMEM)
    scratch = layer_scratch(sz, (4, 4, part))
    for group in (layer_sums(sz), layer_params(sz)):
        scratch.update({name: pltpu.VMEM(*of) for name, of in group.items()})
    scratch.update({"chan_net_%d" % k: of for k, of in enumerate(reduce_scratch(part, width, 2))})
    scratch.update({"tok_net_%d" % k: of for k, of in enumerate(reduce_scratch(pack_rows, sz.lanes, 1))})
    dma = pltpu.SemaphoreType.DMA
    scratch.update(
        pack_all=pltpu.VMEM((2, 4, 4, pack_rows, sz.lanes), BF16),
        vec=pltpu.VMEM((16, sz.channels), F32), vec_in=pltpu.VMEM((3, 16, sz.channels), F32),
        vec_z=pltpu.VMEM((4, 16, sz.channels), F32), own_sem=dma((2,)),
        gather_send=dma((n_gather * 7,)), gather_recv=dma((n_gather * 7,)),
        reduce_send=dma((n_reduce * 7,)), reduce_recv=dma((n_reduce * 7,)),
        vector_send=dma((6,)), vector_recv=dma((6,)),
    )
    return call_kernel(kernel, inputs, outputs, scratch, collective_id=0, has_side_effects=True)


def make_pack(sz, c, vectors, tok_in_part, tok_in_bias, tok_out_part, chan_bias):
    tok_part = tok_in_bias.shape[0]
    runs = sz.channels // 16 // tok_part
    cols = [vector.reshape(runs, tok_part).T for vector in vectors]
    first = jnp.concatenate(
        [tok_in_part.T, tok_in_bias[:, None], jnp.zeros((tok_part, sz.padded - sz.patches - 1), BF16)] + cols, axis=1
    )
    first = jnp.pad(first, ((0, 0), (0, sz.lanes - first.shape[1])))
    second = jnp.pad(tok_out_part, ((0, 0), (0, sz.lanes - sz.patches)))
    rows = -(-(tok_part + sz.hidden // sz.lanes // 2) // 16) * 16
    me = lax.broadcasted_iota(jnp.int32, (16, 1), 0) == lax.axis_index("dp")
    placed = jnp.where(me, chan_bias[None, :], jnp.zeros((), BF16)).reshape(-1, sz.lanes)
    half = placed.shape[0] // 2
    chosen = jnp.where(c == 0, first, second)
    bias = jnp.where(c == 0, placed[:half], placed[half:])
    return jnp.pad(jnp.concatenate([chosen, bias], axis=0), ((0, rows - tok_part - half), (0, 0)))


def unpack(sz, layer, pack_all, tok_part):
    pad, lanes, ch = sz.padded, sz.lanes, sz.channels
    rows = pack_all.shape[3]
    both = [pack_all[m].reshape(16, rows, lanes).astype(F32) for m in range(2)]
    first, second = (value[:, :tok_part].reshape(sz.token_hidden, lanes) for value in both)
    layer.tok_in_t[...] = first[:, :pad].astype(BF16)
    layer.tok_out[...] = second[:, :pad].astype(BF16)
    column = lax.broadcasted_iota(jnp.int32, first.shape, 1)
    layer.tok_in[...] = jnp.transpose(jnp.where(column < sz.patches, first, 0.0))[:pad].astype(BF16)
    layer.tok_out_t[...] = jnp.transpose(jnp.where(column < sz.patches, second, 0.0))[:pad].astype(BF16)
    runs = ch // 16 // tok_part
    shape = (16, tok_part, ch)
    device, row, lane = (lax.broadcasted_iota(jnp.int32, shape, k) for k in range(3))
    for v, ref in enumerate((layer.gain1, layer.shift1, layer.gain2, layer.shift2, layer.out_bias)):
        ref[...] = jnp.zeros_like(ref)
    for h in range(runs):
        place = lane == device * (runs * tok_part) + h * tok_part + row
        chosen = jnp.where(place, 1.0, 0.0).reshape(sz.token_hidden, ch).astype(BF16)
        spread = dot(first.astype(BF16), chosen, TN)
        for v, ref in enumerate((layer.gain1, layer.shift1, layer.gain2, layer.shift2, layer.out_bias)):
            index = pad + v * runs + h
            ref[...] += spread[index : index + 1]
    half = sz.hidden // lanes // 2
    bias = [jnp.sum(value[:, tok_part:], axis=0) for value in both]
    per_block = sz.width // lanes
    for j in range(sz.blocks):
        pieces = []
        for q in range(j * per_block, (j + 1) * per_block):
            pieces.append(bias[q // half][q % half : q % half + 1])
        layer.chan_in_bias[j] = jnp.concatenate(pieces, axis=1)


def local(sz, keep, patches, grad_out, weights, tok_out_bias, params):
    def kernel(refs):
        layer = Layer(sz, **refs)
        gw_slot, gw_sem = refs["gw_slot"], refs["gw_sem"]

        def columns(j):
            return pl.ds(pl.multiple_of(j * sz.width, sz.width), sz.width)

        def weight_loads(j, slot):
            return [
                pltpu.make_async_copy(refs["weights"].at[m, :, columns(j)], layer.w_slot.at[slot, m], layer.w_sem.at[slot, m])
                for m in range(2)
            ]

        def grad_stores(j, m):
            return [pltpu.make_async_copy(gw_slot.at[m], refs["g_weights"].at[m, :, columns(j)], gw_sem.at[m])]

        layer.begin()
        start(weight_loads(0, 0))
        layer.clear()
        lax.fori_loop(0, sz.pairs, layer.mask_pair, 0)
        lax.fori_loop(0, sz.pairs, layer.norm_pair, 0)

        def forward_step(pair, carry):
            layer.token_forward(pair)
            return carry

        lax.fori_loop(0, sz.pairs, forward_step, 0)
        layer.token_forward_end()

        def block_step(j, carry):
            slot = lax.rem(j, 2)
            wait(weight_loads(j, slot))

            @pl.when(j + 1 < sz.blocks)
            def _():
                start(weight_loads(j + 1, 1 - slot))

            def chunk(r, carry):
                layer.row_chunk(j, slot, r)
                return carry

            lax.fori_loop(0, sz.chunks, chunk, 0)
            for m in range(2):

                @pl.when(j >= 1)
                def _():
                    wait(grad_stores(j - 1, m))

                gw_slot[m] = layer.weight_grad(m)
                start(grad_stores(j, m))
            return carry

        lax.fori_loop(0, sz.blocks, block_step, 0)
        for m in range(2):
            wait(grad_stores(sz.blocks - 1, m))
        start(layer.back_copies(0, 0))

        def backward_step(pair, carry):
            layer.token_backward(pair)
            return carry

        lax.fori_loop(0, sz.pairs, backward_step, 0)
        layer.token_backward_end()

    inputs = dict(
        keep=(keep, SMEM), patches=(patches, ANYWHERE), grad_out=(grad_out, ANYWHERE), weights=(weights, ANYWHERE),
        tok_out_bias=(tok_out_bias, VMEM),
    )
    inputs.update({name: (params[name], VMEM) for name in layer_params(sz)})
    outputs = {name: (of, ANYWHERE) for name, of in layer_results(sz).items()}
    outputs["g_weights"] = (((2, sz.channels, sz.hidden), F32), ANYWHERE)
    outputs.update({name: (of, VMEM) for name, of in layer_sums(sz).items()})
    scratch = layer_scratch(sz, (sz.channels,))
    scratch.update(gw_slot=pltpu.VMEM((2, sz.channels, sz.width), F32), gw_sem=pltpu.SemaphoreType.DMA((2,)))
    return call_kernel(kernel, inputs, outputs, scratch)


def on_device(
    patches, image_counts, grad_out,
    ln1_gain, ln1_bias, w_token_in, b_token_in, w_token_out, b_token_out,
    ln2_gain, ln2_bias, w_chan_in, b_chan_in, w_chan_out, b_chan_out,
):
    images, patch, ch = patches.shape
    token_part, hidden_part, part = b_token_in.shape[0], b_chan_in.shape[0], ln1_gain.shape[0]
    n_dp = lax.axis_size("dp")
    hidden = w_chan_in.shape[1]
    sz = Sizes(images, patch, ch, token_part * n_dp, hidden, 512, images * (-(-patch // 8) * 8) // 3)
    pad = sz.padded
    keep = (jnp.arange(images, dtype=jnp.int32) < image_counts[0]).astype(F32)
    tok_out_bias = jnp.pad(b_token_out.astype(F32), (0, pad - patch))[:, None]
    vectors = (ln1_gain, ln1_bias, ln2_gain, ln2_bias, b_chan_out)

    def own(vector, length):
        return lax.dynamic_slice_in_dim(vector, lax.axis_index("dp") * length, length)

    if n_dp == 16 and sz.pairs == 6 and part % 16 == 0 and token_part % 8 == 0 and part % token_part == 0:
        c = lax.axis_index("outer")
        own_weight = jnp.where(c == 0, w_chan_in, w_chan_out.T)
        own_pack = make_pack(sz, c, vectors, w_token_in, b_token_in, w_token_out, b_chan_in)
        res = networked(sz, keep, patches, grad_out, own_weight, own_pack, tok_out_bias)
        g_weights, g_tokens, vec = res["own_out"], res["tok_fin"][:, :token_part], res["vec_out"]
        g_vec = [own(vec[k], part) for k in range(5)]
        g_chan_bias = own(vec[5 : 5 + sz.blocks, : sz.width].reshape(-1), hidden_part)
        g_tok_out_bias = vec[5 + sz.blocks, :patch]
    else:
        weights = lax.all_gather(jnp.stack([w_chan_in, w_chan_out.T]), "dp", axis=1, tiled=True)
        tokens = lax.all_gather(jnp.stack([w_token_in.T, w_token_out]), "dp", axis=1, tiled=True)
        tokens = jnp.pad(tokens, ((0, 0), (0, 0), (0, pad - patch)))
        every = lax.all_gather(jnp.concatenate(vectors + (b_token_in, b_chan_in)), "dp", axis=0)
        whole = [every[:, k * part : (k + 1) * part].reshape(1, ch).astype(F32) for k in range(5)]
        tok_bias = every[:, 5 * part : 5 * part + token_part].reshape(-1)
        params = dict(zip(("gain1", "shift1", "gain2", "shift2", "out_bias"), whole))
        params.update(
            tok_in_t=tokens[0].at[:, patch].set(tok_bias), tok_in=tokens[0].T,
            tok_out_t=tokens[1].T, tok_out=tokens[1],
            chan_in_bias=every[:, 5 * part + token_part :].reshape(sz.blocks, 1, sz.width).astype(F32),
        )
        res = local(sz, keep, patches, grad_out, weights, tok_out_bias, params)
        g_weights = lax.psum_scatter(res["g_weights"].astype(BF16), "dp", scatter_dimension=1, tiled=True)
        g_weights = lax.psum(g_weights, "outer").astype(F32)
        g_tokens = lax.psum(lax.psum_scatter(res["g_tok"], "dp", scatter_dimension=1, tiled=True), "outer")
        sums = [jnp.sum(res[name], axis=0) for name in ("g_gain1", "g_shift1", "g_gain2", "g_shift2", "g_out_bias")]
        sums += [jnp.sum(res["g_chan_in_bias"], axis=1).reshape(-1), res["g_tok_out_bias"][:patch, 0]]
        sums = lax.psum(tuple(sums), ("dp", "outer"))
        g_vec = [own(vector, part) for vector in sums[:5]]
        g_chan_bias, g_tok_out_bias = own(sums[5], hidden_part), sums[6]

    return (
        res["mixed"], res["grad_patches"],
        g_vec[0], g_vec[1], g_tokens[0, :, :patch].T, g_tokens[0, :, patch], g_tokens[1, :, :patch], g_tok_out_bias,
        g_vec[2], g_vec[3], g_weights[0], g_chan_bias, g_weights[1].T, g_vec[4],
    )


def solution(mesh):
    slots = P(("dp", "outer"), None, None)
    return jax.shard_map(
        on_device,
        mesh=mesh,
        in_specs=(
            slots, P(("dp", "outer")), slots, P("dp"), P("dp"), P(None, "dp"), P("dp"), P("dp", None), P(),
            P("dp"), P("dp"), P("dp", None), P("dp"), P(None, "dp"), P("dp"),
        ),
        out_specs=(
            slots, slots, P("dp"), P("dp"), P(None, "dp"), P("dp"), P("dp", None), P(),
            P("dp"), P("dp"), P("dp", None), P("dp"), P(None, "dp"), P("dp"),
        ),
        check_vma=False,
    )
```

```python
import functools
import types

import jax
import jax.numpy as jnp
from jax import lax
from jax.experimental import pallas as pl
from jax.experimental.pallas import tpu as pltpu
from jax.sharding import PartitionSpec as P

EPS = 1e-06
F32 = jnp.float32
BF16 = jnp.bfloat16
NN = (((1,), (0,)), ((), ()))
NT = (((1,), (1,)), ((), ()))
TN = (((0,), (0,)), ((), ()))
MESH = pl.DeviceIdType.MESH
ROOT = 0.7978845608028654
CUBE = 0.044715 * ROOT


def dot(left, right, dims):
    return lax.dot_general(left, right, dims, preferred_element_type=F32)


def gelu_both(value):
    square = value * value
    half = 0.5 + 0.5 * jnp.tanh(value * (ROOT + CUBE * square))
    slope = half + (half - half * half) * (value * (2 * ROOT + 6 * CUBE * square))
    return value * half, slope


def fold(values):
    return jnp.sum(values.reshape(values.shape[0] // 8, 8, values.shape[1]), axis=0)


def lane_mean(values):
    return jnp.mean(values, axis=-1, keepdims=True)


def standardize(values):
    centered = values - lane_mean(values)
    scale = lax.rsqrt(lane_mean(centered * centered) + EPS)
    return centered * scale, scale


def pad_rows(values, rows):
    extra = rows - values.shape[0]
    if extra == 0:
        return values
    return jnp.concatenate([values, jnp.zeros((extra, values.shape[1]), values.dtype)], axis=0)


class Sizes:
    def __init__(self, images, patches, channels, token_hidden, hidden, width, rows):
        self.images, self.patches, self.channels = images, patches, channels
        self.token_hidden, self.hidden, self.width = token_hidden, hidden, width
        self.padded = -(-patches // 8) * 8
        self.flat = images * self.padded
        self.blocks = hidden // width
        self.rows = rows
        self.chunks = self.flat // rows
        self.pairs = images // 2
        self.lanes = -(-self.padded // 128) * 128


def start(copies):
    for copy in copies:
        copy.start()


def wait(copies):
    for copy in copies:
        copy.wait()


class Place:
    def __init__(self):
        me, c = lax.axis_index("dp"), lax.axis_index("outer")
        z = me // 4
        yx = me - 4 * z
        y = yx // 2
        x = yx - 2 * y
        step_x, step_y = 1 - 2 * x, 2 * (1 - 2 * y)
        self.c, self.z, self.yx = c, z, yx
        self.yx_a = yx + (1 - c) * step_x + c * step_y
        self.yx_b = yx + c * step_x + (1 - c) * step_y
        self.yx_ab = yx + step_x + step_y
        self.sibling = (me, 1 - c)
        self.peer_a, self.peer_b = (4 * z + self.yx_a, c), (4 * z + self.yx_b, c)
        self.z_of = [lax.rem(z + k, 4) for k in range(4)]
        self.peer_z = [(4 * self.z_of[k] + yx, c) for k in range(4)]
        self.peers_xy = [self.peer_a, self.peer_b, (4 * z + self.yx_ab, c)]
        self.yx_xy = [self.yx_a, self.yx_b, self.yx_ab]

    def greet(self):
        barrier = pltpu.get_barrier_semaphore()
        peers = [self.sibling] + self.peers_xy + self.peer_z[1:]
        for peer in peers:
            pl.semaphore_signal(barrier, inc=1, device_id=peer, device_id_type=MESH)
        pl.semaphore_wait(barrier, len(peers))


def remote(source, target, sems, index, peer):
    return pltpu.make_async_remote_copy(
        src_ref=source, dst_ref=target, send_sem=sems[0].at[index], recv_sem=sems[1].at[index],
        device_id=peer, device_id_type=MESH,
    )


class Gather:
    def __init__(self, place, own, view, sems, base):
        self.place, self.own, self.view, self.sems, self.base = place, own, view, sems, base

    def send(self, position, index, peer):
        ref = self.view(self.place.c, slice(None), position)
        return remote(ref, ref, self.sems, self.base + index, peer)

    @property
    def along_z(self):
        place = self.place
        target = self.view(place.c, place.z, place.yx)
        return [remote(self.own, target, self.sems, self.base + k - 1, place.peer_z[k]) for k in (1, 2, 3)]

    @property
    def along_a(self):
        return [self.send(self.place.yx, 3, self.place.peer_a)]

    @property
    def along_b(self):
        place = self.place
        return [self.send(place.yx, 4, place.peer_b), self.send(place.yx_a, 5, place.peer_b)]

    @property
    def along_xy(self):
        place = self.place
        return [self.send(place.yx, 3 + k, place.peers_xy[k]) for k in range(3)]

    @property
    def swap(self):
        return [self.send(slice(None), 6, self.place.sibling)]

    def to_xy(self):
        wait(self.along_z)
        start(self.along_xy)

    def xy_to_sibling(self):
        wait(self.along_xy)
        start(self.swap)

    def to_a(self):
        wait(self.along_z)
        start(self.along_a)

    def to_b(self):
        wait(self.along_a)
        start(self.along_b)

    def to_sibling(self):
        wait(self.along_b)
        start(self.swap)


class Reduce:
    def __init__(self, place, refs, own_out, sems, base, slot):
        (self.mine, csend, crecv, self.send1, self.keep1, recv1, self.send2, self.keep2, recv2,
         self.send3, self.keep3, recv3) = refs
        self.place, self.own_out, self.csend, self.sems, self.base = place, own_out, csend, sems, base
        self.crecv, self.recv1, self.recv2, self.recv3 = crecv.at[slot], recv1.at[slot], recv2.at[slot], recv3.at[slot]

    def send(self, source, target, index, peer):
        return remote(source, target, self.sems, self.base + index, peer)

    @property
    def swap(self):
        return [self.send(self.csend, self.crecv, 0, self.place.sibling)]

    @property
    def along_b(self):
        return [self.send(self.send1, self.recv1, 1, self.place.peer_b)]

    @property
    def along_a(self):
        return [self.send(self.send2, self.recv2, 2, self.place.peer_a)]

    @property
    def along_z(self):
        place = self.place
        return [
            self.send(self.send3.at[place.z_of[k]], self.recv3.at[k - 1], 2 + k, place.peer_z[k]) for k in (1, 2, 3)
        ]

    @property
    def finish(self):
        return [self.send(self.own_out, self.own_out, 6, self.place.sibling)]

    def to_b(self):
        wait(self.swap)
        place = self.place

        def step(z, carry):
            for q, (kept, sent) in enumerate(((place.yx, place.yx_b), (place.yx_a, place.yx_ab))):
                self.keep1[z, q] = (self.mine[z, kept].astype(F32) + self.crecv[z, kept].astype(F32)).astype(BF16)
                self.send1[z, q] = (self.mine[z, sent].astype(F32) + self.crecv[z, sent].astype(F32)).astype(BF16)
            return carry

        lax.fori_loop(0, 4, step, 0)
        start(self.along_b)

    def to_a(self):
        wait(self.along_b)

        def step(z, carry):
            self.keep2[z] = self.keep1[z, 0].astype(F32) + self.recv1[z, 0].astype(F32)
            self.send2[z] = (self.keep1[z, 1].astype(F32) + self.recv1[z, 1].astype(F32)).astype(BF16)
            return carry

        lax.fori_loop(0, 4, step, 0)
        start(self.along_a)

    def to_z(self):
        wait(self.along_a)

        def step(z, carry):
            self.send3[z] = (self.keep2[z] + self.recv2[z].astype(F32)).astype(BF16)
            return carry

        lax.fori_loop(0, 4, step, 0)
        z = self.place.z
        self.keep3[...] = self.keep2[z] + self.recv2[z].astype(F32)
        start(self.along_z)

    def to_owner(self):
        wait(self.along_z)
        total = self.keep3[...]
        for k in range(3):
            total += self.recv3[k].astype(F32)
        self.own_out[...] = total
        start(self.finish)


class SmallReduce:
    def __init__(self, place, refs, own_out, sems):
        self.mine, self.csend, self.crecv, self.send1, self.keep1, self.recv1, self.send3, self.keep3, self.recv3 = refs
        self.place, self.own_out, self.sems = place, own_out, sems

    def send(self, source, target, index, peer):
        return remote(source, target, self.sems, index, peer)

    @property
    def swap(self):
        return [self.send(self.csend, self.crecv, 0, self.place.sibling)]

    @property
    def along_xy(self):
        place = self.place
        return [self.send(self.send1.at[k], self.recv1.at[k], 1 + k, place.peers_xy[k]) for k in range(3)]

    @property
    def along_z(self):
        place = self.place
        return [
            self.send(self.send3.at[place.z_of[k]], self.recv3.at[k - 1], 3 + k, place.peer_z[k]) for k in (1, 2, 3)
        ]

    @property
    def finish(self):
        return [self.send(self.own_out, self.own_out, 7, self.place.sibling)]

    def to_xy(self):
        wait(self.swap)
        place = self.place
        for k in range(3):
            at = place.yx_xy[k]
            self.send1[k] = (self.mine[:, at] + self.crecv[:, at].astype(F32)).astype(BF16)
        start(self.along_xy)
        self.keep1[...] = self.mine[:, place.yx] + self.crecv[:, place.yx].astype(F32)

    def to_z(self):
        wait(self.along_xy)
        total = self.keep1[...]
        for k in range(3):
            total += self.recv1[k].astype(F32)
        self.send3[...] = total.astype(BF16)
        start(self.along_z)
        self.keep1[...] = total
        self.keep3[...] = self.keep1[self.place.z]

    def to_owner(self):
        wait(self.along_z)
        total = self.keep3[...]
        for k in range(3):
            total += self.recv3[k].astype(F32)
        self.own_out[...] = total
        start(self.finish)


def small_reduce_scratch(part, width):
    return [
        pltpu.VMEM((4, 4, part, width), F32),
        pltpu.VMEM((4, 4, part, width), BF16), pltpu.VMEM((4, 4, part, width), BF16),
        pltpu.VMEM((3, 4, part, width), BF16), pltpu.VMEM((4, part, width), F32),
        pltpu.VMEM((3, 4, part, width), BF16),
        pltpu.VMEM((4, part, width), BF16), pltpu.VMEM((part, width), F32),
        pltpu.VMEM((3, part, width), BF16),
    ]


def reduce_scratch(part, width, slots):
    return [
        pltpu.VMEM((4, 4, part, width), BF16),
        pltpu.VMEM((4, 4, part, width), BF16), pltpu.VMEM((slots, 4, 4, part, width), BF16),
        pltpu.VMEM((4, 2, part, width), BF16), pltpu.VMEM((4, 2, part, width), BF16),
        pltpu.VMEM((slots, 4, 2, part, width), BF16),
        pltpu.VMEM((4, part, width), BF16), pltpu.VMEM((4, part, width), F32),
        pltpu.VMEM((slots, 4, part, width), BF16),
        pltpu.VMEM((4, part, width), BF16), pltpu.VMEM((part, width), F32),
        pltpu.VMEM((slots, 3, part, width), BF16),
    ]


class Layer:
    def __init__(self, sz, refs):
        self.sz = sz
        self.__dict__.update(vars(refs))

    def load_copies(self, pair, slot):
        return [
            pltpu.make_async_copy(self.patches.at[pair * 2 + k], self.x_slot.at[slot, k], self.load_sem.at[slot, k])
            for k in range(2)
        ]

    def next_images(self, pair):
        slot = lax.rem(pair, 2)
        following = jnp.where(pair + 1 < self.sz.pairs, pair + 1, 0)
        start(self.load_copies(following, 1 - slot))
        wait(self.load_copies(pair, slot))

    def image_of(self, pair, k):
        return pad_rows(self.x_slot[lax.rem(pair, 2), k].astype(F32), self.sz.padded)

    def cotangent_copies(self, pair, slot):
        return [
            pltpu.make_async_copy(self.grad_out.at[pair * 2 + k], self.mixed_slot.at[slot, k], self.out_sem.at[slot, k, 0])
            for k in range(2)
        ]

    def keep_copies(self, pair, slot, k):
        i = pair * 2 + k
        return [
            pltpu.make_async_copy(self.act_slot.at[slot, k], self.kept_act.at[i], self.act_sem.at[slot, k, 0]),
            pltpu.make_async_copy(self.slope_slot.at[slot, k], self.kept_slope.at[i], self.act_sem.at[slot, k, 1]),
        ]

    def back_copies(self, pair, slot):
        copies = []
        for k in range(2):
            i = pair * 2 + k
            copies += [
                pltpu.make_async_copy(self.kept_act.at[i], self.act_slot.at[slot, k], self.act_sem.at[slot, k, 0]),
                pltpu.make_async_copy(self.kept_slope.at[i], self.slope_slot.at[slot, k], self.act_sem.at[slot, k, 1]),
            ]
        return copies

    def result_copies(self, pair, slot, k):
        i = pair * 2 + k
        return [
            pltpu.make_async_copy(self.gp_slot.at[slot, k], self.grad_patches.at[i], self.out_sem.at[slot, k, 1]),
        ]

    def begin(self):
        start(self.load_copies(0, 0))
        start(self.cotangent_copies(0, 0))

    def clear(self):
        for ref in (self.g_gain1, self.g_shift1, self.g_gain2, self.g_shift2, self.g_out_bias, self.g_tok_out_bias,
                    self.g_tok, self.g_chan_in_bias):
            ref[...] = jnp.zeros_like(ref)

    def kept(self, i):
        return jnp.where(i < self.counts[0], 1.0, 0.0)

    def both(self, pair):
        return pl.ds(pl.multiple_of(pair * 2 * self.sz.padded, 16), 2 * self.sz.padded)

    def image(self, i):
        return pl.ds(pl.multiple_of(i * self.sz.padded, 8), self.sz.padded)

    def mask_pair(self, pair, carry):
        sz, slot = self.sz, lax.rem(pair, 2)

        @pl.when(pair + 1 < sz.pairs)
        def _():
            start(self.cotangent_copies(pair + 1, 1 - slot))

        wait(self.cotangent_copies(pair, slot))
        cotangent = jnp.concatenate(
            [pad_rows(self.mixed_slot[slot, k].astype(F32), sz.padded) * self.kept(pair * 2 + k) for k in range(2)],
            axis=0,
        )
        self.lhs[1, self.both(pair), :] = cotangent.astype(BF16)
        self.g_out_bias[...] += fold(cotangent)
        return carry

    def norm_pair(self, pair, carry):
        self.next_images(pair)
        for k in range(2):
            xhat, _ = standardize(self.image_of(pair, k))
            self.total_din[self.image(pair * 2 + k), :] = xhat
        return carry

    def token_input(self, xhat):
        patch = self.sz.patches
        value = xhat * self.gain1[...] + self.shift1[...]
        whole = patch // 8 * 8
        rest = value[whole:]
        row = lax.broadcasted_iota(jnp.int32, rest.shape, 0) + whole
        rest = jnp.where(row < patch, rest, jnp.where(row == patch, 1.0, 0.0))
        return jnp.concatenate([value[:whole], rest], axis=0).astype(BF16)

    def token_forward(self, pair):
        sz, slot = self.sz, lax.rem(pair, 2)

        @pl.when(pair >= 2)
        def _():
            for k in range(2):
                wait(self.keep_copies(pair - 2, slot, k))

        self.next_images(pair)
        both = self.both(pair)
        residuals = []
        for k in range(2):
            i = pair * 2 + k
            token_in = self.token_input(self.total_din[self.image(i), :])
            act, slope = gelu_both(dot(self.tok_in_t[...], token_in, NN))
            act = act.astype(BF16)
            self.act_slot[slot, k] = act
            self.slope_slot[slot, k] = slope.astype(BF16)
            residuals.append(self.image_of(pair, k) + dot(self.tok_out_t[...], act, NN) + self.tok_out_bias[...])
        residual = jnp.concatenate(residuals, axis=0)
        hat, scale = standardize(residual)
        self.lhs[0, both, :] = (hat * self.gain2[...] + self.shift2[...]).astype(BF16)
        self.xhat2[both, :] = hat.astype(BF16)
        lane = lax.broadcasted_iota(jnp.int32, self.scale2.shape, 1)
        self.scale2[...] = jnp.where(lane == pair, scale, self.scale2[...])
        self.total_out[both, :] = residual + self.out_bias[...]
        self.total_din[both, :] = jnp.zeros((2 * sz.padded, sz.channels), F32)
        for k in range(2):
            start(self.keep_copies(pair, slot, k))

    def token_forward_end(self):
        for pair in range(max(0, self.sz.pairs - 2), self.sz.pairs):
            for k in range(2):
                wait(self.keep_copies(pair, pair % 2, k))

    def weights_of(self, slot, matrix):
        return self.w_slot[slot, matrix].reshape(self.sz.channels, self.sz.width)

    def row_chunk(self, j, slot, r, late):
        sz = self.sz
        rows = pl.ds(pl.multiple_of(r * sz.rows, 16), sz.rows)
        w_in, w_out = self.weights_of(slot, 0), self.weights_of(slot, 1)
        pre = dot(self.lhs[0, rows, :], w_in, NN) + self.chan_in_bias[j]
        d_act = dot(self.lhs[1, rows, :], w_out, NN)
        act, slope = gelu_both(pre)
        act = act.astype(BF16)
        d_pre = d_act * slope
        self.g_chan_in_bias[j] += fold(d_pre)
        d_pre = d_pre.astype(BF16)
        self.rhs[1 + slot, rows, :] = act
        self.rhs[0, rows, :] = d_pre
        if not late:
            self.total_out[rows, :] += dot(act, w_out, NT)
        self.total_din[rows, :] += dot(d_pre, w_in, NT)

    def weight_grad(self, matrix, slot):
        return dot(self.lhs[matrix], self.rhs[matrix * (1 + slot)], TN)

    def mixed_copies(self, pair, slot):
        return [
            pltpu.make_async_copy(self.mixed_slot.at[slot, k], self.mixed.at[pair * 2 + k], self.out_sem.at[slot, k, 0])
            for k in range(2)
        ]

    def finish_output(self, pair):
        sz, slot = self.sz, lax.rem(pair, 2)

        @pl.when(pair >= 2)
        def _():
            wait(self.mixed_copies(pair - 2, slot))

        both = self.both(pair)
        total = self.total_out[both, :]
        for late in range(2):
            total += dot(self.rhs[1 + late, both, :], self.weights_of(late, 1), NT)
        for k in range(2):
            layer = total[k * sz.padded : k * sz.padded + sz.padded] * self.kept(pair * 2 + k)
            self.mixed_slot[slot, k] = layer[: sz.patches].astype(BF16)
        start(self.mixed_copies(pair, slot))

    def finish_output_end(self):
        for pair in range(self.sz.pairs - 2, self.sz.pairs):
            wait(self.mixed_copies(pair, pair % 2))

    def token_backward(self, pair):
        sz, slot = self.sz, lax.rem(pair, 2)
        pad = sz.padded

        @pl.when(pair + 1 < sz.pairs)
        def _():
            start(self.back_copies(pair + 1, 1 - slot))

        @pl.when(pair >= 2)
        def _():
            for k in range(2):
                wait(self.result_copies(pair - 2, slot, k))

        self.next_images(pair)
        both = self.both(pair)
        d_in = self.total_din[both, :]
        hat = self.xhat2[both, :].astype(F32)
        self.g_gain2[...] += fold(d_in * hat)
        self.g_shift2[...] += fold(d_in)
        e = d_in * self.gain2[...]
        lane = lax.broadcasted_iota(jnp.int32, self.scale2.shape, 1)
        scale2 = jnp.sum(jnp.where(lane == pair, self.scale2[...], 0.0), axis=-1, keepdims=True)
        d_residual = self.lhs[1, both, :].astype(F32) + scale2 * (
            e - lane_mean(e) - hat * lane_mean(e * hat)
        )
        rounded = d_residual.astype(BF16).astype(F32)
        wait(self.back_copies(pair, slot))
        for k in range(2):
            i = pair * 2 + k
            part = slice(k * pad, (k + 1) * pad)
            d_token_out = rounded[part].astype(BF16)
            self.g_tok[1] += dot(self.act_slot[slot, k], d_token_out, NT)
            self.g_tok_out_bias[...] += jnp.sum(rounded[part], axis=-1, keepdims=True)
            d_pre = dot(self.tok_out[...], d_token_out, NN) * self.slope_slot[slot, k].astype(F32)
            d_pre = d_pre.astype(BF16)
            hat1, scale1 = standardize(self.image_of(pair, k))
            self.g_tok[0] += dot(d_pre, self.token_input(hat1), NT)
            d_token_in = dot(self.tok_in[...], d_pre, NN)
            self.g_gain1[...] += fold(d_token_in * hat1)
            self.g_shift1[...] += fold(d_token_in)
            f = d_token_in * self.gain1[...]
            result = d_residual[part] + scale1 * (f - lane_mean(f) - hat1 * lane_mean(f * hat1))
            self.gp_slot[slot, k] = result[: sz.patches].astype(BF16)
            start(self.result_copies(pair, slot, k))

    def token_backward_end(self):
        wait(self.load_copies(0, self.sz.pairs % 2))
        for pair in range(max(0, self.sz.pairs - 2), self.sz.pairs):
            for k in range(2):
                wait(self.result_copies(pair, pair % 2, k))


def layer_scratch(sz, weight_shape):
    images, patch, ch = sz.images, sz.patches, sz.channels
    return dict(
        x_slot=pltpu.VMEM((2, 2, patch, ch), BF16),
        lhs=pltpu.VMEM((2, sz.flat, ch), BF16), xhat2=pltpu.VMEM((sz.flat, ch), BF16),
        scale2=pltpu.VMEM((2 * sz.padded, 128), F32),
        total_out=pltpu.VMEM((sz.flat, ch), F32), total_din=pltpu.VMEM((sz.flat, ch), F32),
        act_slot=pltpu.VMEM((2, 2, sz.token_hidden, ch), BF16),
        slope_slot=pltpu.VMEM((2, 2, sz.token_hidden, ch), BF16),
        rhs=pltpu.VMEM((3, sz.flat, sz.width), BF16),
        w_slot=pltpu.VMEM((2, 2) + weight_shape + (sz.width,), BF16),
        mixed_slot=pltpu.VMEM((2, 2, patch, ch), BF16), gp_slot=pltpu.VMEM((2, 2, patch, ch), BF16),
        load_sem=pltpu.SemaphoreType.DMA((2, 2)), act_sem=pltpu.SemaphoreType.DMA((2, 2, 2)),
        w_sem=pltpu.SemaphoreType.DMA((2, 2)), out_sem=pltpu.SemaphoreType.DMA((2, 2, 2)),
    )


def layer_sums(sz):
    ch = sz.channels
    return dict(
        g_gain1=((8, ch), F32), g_shift1=((8, ch), F32), g_gain2=((8, ch), F32), g_shift2=((8, ch), F32),
        g_out_bias=((8, ch), F32), g_tok_out_bias=((sz.padded, 1), F32),
        g_tok=((2, sz.token_hidden, sz.padded), F32), g_chan_in_bias=((sz.blocks, 8, sz.width), F32),
    )


def layer_params(sz):
    ch, pad, th = sz.channels, sz.padded, sz.token_hidden
    return dict(
        gain1=((1, ch), F32), shift1=((1, ch), F32), gain2=((1, ch), F32), shift2=((1, ch), F32),
        out_bias=((1, ch), F32), tok_in_t=((th, pad), BF16), tok_in=((pad, th), BF16),
        tok_out_t=((pad, th), BF16), tok_out=((th, pad), BF16), chan_in_bias=((sz.blocks, 1, sz.width), F32),
    )


def layer_results(sz):
    return dict(
        mixed=((sz.images, sz.patches, sz.channels), BF16),
        grad_patches=((sz.images, sz.patches, sz.channels), BF16),
        kept_act=((sz.images, sz.token_hidden, sz.channels), BF16),
        kept_slope=((sz.images, sz.token_hidden, sz.channels), BF16),
    )


def call_kernel(kernel, inputs, outputs, scratch, vmem_mib, **params):
    names = list(inputs) + list(outputs) + list(scratch)

    def body(*refs):
        kernel(types.SimpleNamespace(**dict(zip(names, refs))))

    results = pl.pallas_call(
        body,
        out_shape=[jax.ShapeDtypeStruct(*of) for of, _ in outputs.values()],
        in_specs=[spec for _, spec in inputs.values()],
        out_specs=[spec for _, spec in outputs.values()],
        scratch_shapes=list(scratch.values()),
        compiler_params=pltpu.CompilerParams(vmem_limit_bytes=vmem_mib * 2**20, **params),
    )(*[array for array, _ in inputs.values()])
    return types.SimpleNamespace(**dict(zip(outputs, results)))


ANYWHERE = pl.BlockSpec(memory_space=pl.ANY)
VMEM = pl.BlockSpec(memory_space=pltpu.VMEM)
SMEM = pl.BlockSpec(memory_space=pltpu.SMEM)


def networked(sz, counts, patches, grad_out, **params):
    part = sz.channels // 16
    tok_part = sz.token_hidden // 16
    pack_rows = -(-(tok_part + 1) // 16) * 16
    blocks, width = sz.blocks, sz.width
    n_gather, n_reduce = blocks + 1, blocks

    def kernel(refs):
        place = Place()
        layer = Layer(sz, refs)
        gathered, pack_all = refs.gathered, refs.pack_all
        gather_sems = (refs.gather_send, refs.gather_recv)
        reduce_sems = (refs.reduce_send, refs.reduce_recv)
        vector_sems = (refs.vector_send, refs.vector_recv)
        own_out, tok_fin = refs.own_out, refs.tok_fin
        c = place.c
        chan_refs = [getattr(refs, "c%d" % k) for k in range(12)]
        tok_refs = [getattr(refs, "t%d" % k) for k in range(9)]

        def columns(j):
            return pl.ds(pl.multiple_of(j * width, width), width)

        def gather(j):
            cols = columns(j)

            def view(matrix, z, yx):
                return gathered.at[matrix, z, yx, :, cols]

            return Gather(place, refs.own_weight.at[:, cols], view, gather_sems, j * 7)

        def pack_view(matrix, z, yx):
            return pack_all.at[matrix, z, yx]

        pack = Gather(place, refs.pack_own, pack_view, gather_sems, blocks * 7)

        def reduce(j):
            return Reduce(place, chan_refs, own_out.at[c, :, columns(j)], reduce_sems, j * 7, lax.rem(j, 2))

        tok_reduce = SmallReduce(place, tok_refs, tok_fin.at[c], (refs.tok_send, refs.tok_recv))

        def own_load(source):
            return [pltpu.make_async_copy(source, refs.own_weight, refs.own_sem.at[2])]

        own_copies = [
            pltpu.make_async_copy(refs.own_weight, gathered.at[c, place.z, place.yx], refs.own_sem.at[0]),
            pltpu.make_async_copy(refs.pack_own, pack_all.at[c, place.z, place.yx], refs.own_sem.at[1]),
        ]

        def weight_loads(j, slot):
            return [
                pltpu.make_async_copy(
                    gathered.at[m, :, :, :, columns(j)], layer.w_slot.at[slot, m], layer.w_sem.at[slot, m]
                )
                for m in range(2)
            ]

        @pl.when(c == 0)
        def _():
            start(own_load(refs.p_w_chan_in))

        @pl.when(c == 1)
        def _():
            start(own_load(refs.p_w_chan_out))

        layer.begin()
        make_pack(sz, c, refs)
        wait(own_load(refs.p_w_chan_in))
        start(own_copies)
        place.greet()
        start(pack.along_z)
        start(gather(0).along_z)
        layer.clear()
        lax.fori_loop(0, sz.pairs, layer.mask_pair, 0)
        wait(own_copies)
        pack.to_xy()
        lax.fori_loop(0, sz.pairs // 2, layer.norm_pair, 0)
        gather(0).to_a()
        start(gather(1).along_z)
        lax.fori_loop(sz.pairs // 2, sz.pairs, layer.norm_pair, 0)
        pack.xy_to_sibling()
        wait(pack.swap)
        unpack(sz, layer, pack_all, tok_part)
        gather(0).to_b()
        gather(1).to_a()
        start(gather(2).along_z)

        def forward_step(pair, carry):
            layer.token_forward(pair)

            @pl.when(pair == 3)
            def _():
                gather(0).to_sibling()
                gather(1).to_b()
                gather(2).to_a()
                start(gather(3).along_z)

            @pl.when(pair == 5)
            def _():
                wait(gather(0).swap)
                start(weight_loads(0, 0))

            return carry

        lax.fori_loop(0, sz.pairs, forward_step, 0)
        layer.token_forward_end()

        start(layer.back_copies(0, 0))

        def block_step(late, j, carry):
            slot = lax.rem(j, 2)
            wait(weight_loads(j, slot))

            def chunk(r, carry):
                layer.row_chunk(j, slot, r, late)

                @pl.when(r == 0)
                def _():
                    @pl.when(j >= 3)
                    def _():
                        reduce(j - 3).to_owner()

                    @pl.when(j >= 1)
                    def _():
                        reduce(j - 1).to_b()

                @pl.when(r == 1)
                def _():
                    @pl.when(j + 1 < blocks)
                    def _():
                        gather(j + 1).to_sibling()

                    @pl.when(j + 2 < blocks)
                    def _():
                        gather(j + 2).to_b()

                    @pl.when(j + 3 < blocks)
                    def _():
                        gather(j + 3).to_a()

                    @pl.when(j + 4 < blocks)
                    def _():
                        start(gather(j + 4).along_z)

                @pl.when(r == 2)
                def _():
                    @pl.when(j >= 2)
                    def _():
                        reduce(j - 2).to_z()

                return carry

            lax.fori_loop(0, sz.chunks, chunk, 0)
            mine, csend = chan_refs[0], chan_refs[1]
            csend[...] = layer.weight_grad(1 - c, slot).astype(BF16).reshape(csend.shape)
            start(reduce(j).swap)

            @pl.when(j + 1 < blocks)
            def _():
                wait(gather(j + 1).swap)
                start(weight_loads(j + 1, 1 - slot))

            mine[...] = layer.weight_grad(c, slot).astype(BF16).reshape(mine.shape)

            @pl.when(j >= 1)
            def _():
                reduce(j - 1).to_a()

            return carry

        lax.fori_loop(0, blocks - 2, functools.partial(block_step, False), 0)
        lax.fori_loop(blocks - 2, blocks, functools.partial(block_step, True), 0)

        def backward_step(pair, carry):
            layer.token_backward(pair)

            @pl.when(pair == 0)
            def _():
                reduce(blocks - 3).to_owner()
                reduce(blocks - 1).to_b()

            @pl.when(pair == 1)
            def _():
                reduce(blocks - 2).to_z()

            @pl.when(pair == 3)
            def _():
                reduce(blocks - 2).to_owner()
                reduce(blocks - 1).to_a()

            @pl.when(pair == 5)
            def _():
                reduce(blocks - 1).to_z()

            return carry

        lax.fori_loop(0, sz.pairs, backward_step, 0)

        mine, csend = tok_refs[0], tok_refs[1]

        def packed(matrix):
            value = layer.g_tok[matrix].reshape(16, tok_part, sz.padded)
            return value

        filler = jnp.zeros((16, pack_rows - tok_part, sz.padded), F32)
        for ref, matrix in ((csend, 1 - c), (mine, c)):
            value = jnp.concatenate([packed(matrix), filler], axis=1).astype(ref.dtype)
            ref[:, :, :, 0 : sz.padded] = value.reshape(4, 4, pack_rows, sz.padded)
            ref[:, :, :, sz.padded :] = jnp.zeros((4, 4, pack_rows, sz.lanes - sz.padded), ref.dtype)
            if ref is csend:
                start(tok_reduce.swap)
        vec, vec_in, vec_xy, vec_z = refs.vec, refs.vec_in, refs.vec_xy, refs.vec_z
        vec[...] = jnp.zeros_like(vec)
        for k, ref in enumerate((layer.g_gain1, layer.g_shift1, layer.g_gain2, layer.g_shift2, layer.g_out_bias)):
            vec[k : k + 1, :] = jnp.sum(ref[...], axis=0, keepdims=True)
        column = jnp.broadcast_to(layer.g_tok_out_bias[...], (sz.padded, 128))
        vec[5:6, 0 : sz.padded] = jnp.transpose(column)[0:1]
        flat = [jnp.sum(layer.g_chan_in_bias[j], axis=0, keepdims=True) for j in range(blocks)]
        flat = jnp.concatenate(flat, axis=1)
        for k in range(sz.hidden // sz.channels):
            vec[6 + k : 7 + k, :] = flat[:, k * sz.channels : (k + 1) * sz.channels]

        vector_swap = [remote(vec, vec_in, vector_sems, 0, place.sibling)]
        vector_xy = [remote(vec, vec_xy.at[place.yx], vector_sems, 1 + k, place.peers_xy[k]) for k in range(3)]
        vector_z = [remote(vec, vec_z.at[place.z], vector_sems, 3 + k, place.peer_z[k]) for k in (1, 2, 3)]
        def output(pair, carry):
            layer.finish_output(pair)
            return carry

        start(vector_swap)
        reduce(blocks - 1).to_owner()
        lax.fori_loop(0, 1, output, 0)
        tok_reduce.to_xy()
        wait(vector_swap)
        vec[...] += vec_in[...]
        start(vector_xy)
        vec_xy[place.yx] = vec[...]
        lax.fori_loop(1, 4, output, 0)
        tok_reduce.to_z()
        wait(vector_xy)
        vec[...] = (vec_xy[0] + vec_xy[1]) + (vec_xy[2] + vec_xy[3])
        start(vector_z)
        vec_z[place.z] = vec[...]
        lax.fori_loop(4, sz.pairs, output, 0)
        layer.token_backward_end()
        layer.finish_output_end()
        tok_reduce.to_owner()
        wait(vector_z)
        refs.vec_out[...] = (vec_z[0] + vec_z[1]) + (vec_z[2] + vec_z[3])

        def finish(j, carry):
            wait(reduce(j).finish)
            return carry

        lax.fori_loop(0, blocks, finish, 0)
        wait(tok_reduce.finish)

    inputs = dict(counts=(counts, SMEM), patches=(patches, ANYWHERE), grad_out=(grad_out, ANYWHERE))
    inputs.update({"p_" + name: (of, ANYWHERE if name[:6] == "w_chan" else VMEM) for name, of in params.items()})
    outputs = {name: (of, ANYWHERE) for name, of in layer_results(sz).items()}
    outputs.update(
        gathered=(((2, 4, 4, part, sz.hidden), BF16), ANYWHERE), own_out=(((2, part, sz.hidden), F32), VMEM),
        tok_fin=(((2, pack_rows, sz.lanes), F32), VMEM), vec_out=(((16, sz.channels), F32), VMEM),
    )
    scratch = layer_scratch(sz, (4, 4, part))
    for group in (layer_sums(sz), layer_params(sz)):
        scratch.update({name: pltpu.VMEM(*of) for name, of in group.items()})
    scratch.update({"c%d" % k: of for k, of in enumerate(reduce_scratch(part, width, 2))})
    scratch.update({"t%d" % k: of for k, of in enumerate(small_reduce_scratch(pack_rows, sz.lanes))})
    dma = pltpu.SemaphoreType.DMA
    scratch.update(
        pack_all=pltpu.VMEM((2, 4, 4, pack_rows, sz.lanes), BF16), pack_own=pltpu.VMEM((pack_rows, sz.lanes), BF16),
        pack_tmp=pltpu.VMEM((pack_rows, sz.lanes), F32), own_weight=pltpu.VMEM((part, sz.hidden), BF16),
        tok_out_bias=pltpu.VMEM((sz.padded, 1), F32),
        vec=pltpu.VMEM((16, sz.channels), F32), vec_in=pltpu.VMEM((16, sz.channels), F32),
        vec_xy=pltpu.VMEM((4, 16, sz.channels), F32), vec_z=pltpu.VMEM((4, 16, sz.channels), F32), own_sem=dma((3,)),
        gather_send=dma((n_gather * 7,)), gather_recv=dma((n_gather * 7,)),
        reduce_send=dma((n_reduce * 7,)), reduce_recv=dma((n_reduce * 7,)),
        tok_send=dma((8,)), tok_recv=dma((8,)), vector_send=dma((7,)), vector_recv=dma((7,)),
    )
    return call_kernel(kernel, inputs, outputs, scratch, 62, collective_id=0, has_side_effects=True)


def make_pack(sz, c, refs):
    tmp = refs.pack_tmp
    tok_in, tok_out = refs.p_w_token_in, refs.p_w_token_out
    tok_part = tok_out.shape[0]

    def row(*sources):
        values = [source[...].astype(F32)[None, :] for source in sources]
        rest = sz.lanes - sum(value.shape[1] for value in values)
        return jnp.concatenate(values + [jnp.zeros((1, rest), F32)], axis=1)

    tmp[...] = jnp.zeros_like(tmp)
    tmp[0:tok_part, 0 : sz.patches] = jnp.where(c == 0, tok_in[...].astype(F32), tok_out[...].astype(F32))
    first = row(refs.p_ln1_gain, refs.p_ln1_bias, refs.p_ln2_gain, refs.p_ln2_bias, refs.p_b_chan_out)
    tmp[tok_part : tok_part + 1, :] = jnp.where(c == 0, first, row(refs.p_b_chan_in, refs.p_b_token_in))
    refs.pack_own[...] = tmp[...].astype(BF16)
    bias = jnp.broadcast_to(row(refs.p_b_token_out), (8, sz.lanes))
    refs.tok_out_bias[...] = jnp.transpose(bias)[0 : sz.padded, 0:1]


def spread(rows, length, lanes, first_lane, columns):
    at = lax.broadcasted_iota(jnp.int32, (1, columns[1] - columns[0]), 1) + columns[0]
    device = jnp.zeros_like(at)
    for k in range(1, 16):
        device += jnp.where(at >= k * length, 1, 0)
    source = at - device * length + first_lane
    lane = lax.broadcasted_iota(jnp.int32, (lanes, source.shape[1]), 0)
    chosen = jnp.where(lane == source, 1.0, 0.0).astype(BF16)
    value = dot(rows, chosen, NN)
    owner = lax.broadcasted_iota(jnp.int32, value.shape, 0)
    return jnp.sum(jnp.where(owner == device, value, 0.0), axis=0, keepdims=True)


def unpack(sz, layer, pack_all, tok_part):
    pad, lanes, ch = sz.padded, sz.lanes, sz.channels
    rows = pack_all.shape[3]
    both = [pack_all[m].reshape(16, rows, lanes).astype(F32) for m in range(2)]
    first, second = (value[:, :tok_part].reshape(sz.token_hidden, lanes) for value in both)
    vectors, biases = (value[:, tok_part].astype(BF16) for value in both)
    part = ch // 16
    for v, ref in enumerate((layer.gain1, layer.shift1, layer.gain2, layer.shift2, layer.out_bias)):
        ref[...] = spread(vectors, part, lanes, v * part, (0, ch))
    for j in range(sz.blocks):
        layer.chan_in_bias[j] = spread(biases, sz.hidden // 16, lanes, 0, (j * sz.width, (j + 1) * sz.width))
    bias = spread(biases, tok_part, lanes, sz.hidden // 16, (0, sz.token_hidden))
    bias = jnp.transpose(jnp.broadcast_to(bias, (8, sz.token_hidden)))[:, 0:1]
    column = lax.broadcasted_iota(jnp.int32, first.shape, 1)
    layer.tok_in_t[...] = jnp.where(column == sz.patches, bias, first)[:, :pad].astype(BF16)
    layer.tok_out[...] = second[:, :pad].astype(BF16)
    layer.tok_in[...] = jnp.transpose(first)[:pad].astype(BF16)
    layer.tok_out_t[...] = jnp.transpose(second)[:pad].astype(BF16)


def hand_out(sz, raw, tok_part, hidden_part):
    part = raw.own_out.shape[1]
    images, patch, ch = sz.images, sz.patches, sz.channels

    def kernel(refs):
        load_sem, store_sem, own_sem = refs.load_sem, refs.store_sem, refs.own_sem

        def loads(i):
            return [
                pltpu.make_async_copy(refs.raw_mixed.at[i], refs.tmp_mixed.at[i], load_sem.at[0, i]),
                pltpu.make_async_copy(refs.raw_grad.at[i], refs.tmp_grad.at[i], load_sem.at[1, i]),
            ]

        def stores(i):
            return [
                pltpu.make_async_copy(refs.tmp_mixed.at[i], refs.mixed.at[i], store_sem.at[0, i]),
                pltpu.make_async_copy(refs.tmp_wide.at[i], refs.grad_patches.at[i], store_sem.at[1, i]),
            ]

        def load(i, carry):
            start(loads(i))
            return carry

        def store(i, carry):
            wait(loads(i))
            refs.tmp_wide[i] = refs.tmp_grad[i].astype(F32)
            start(stores(i))
            return carry

        def finish(i, carry):
            wait(stores(i))
            return carry

        own_loads = [pltpu.make_async_copy(refs.own, refs.tmp_own, own_sem.at[0])]
        own_stores = [
            pltpu.make_async_copy(refs.tmp_own.at[m], target, own_sem.at[1 + m])
            for m, target in enumerate((refs.g_chan_in, refs.g_chan_out))
        ]
        lax.fori_loop(0, images, load, 0)
        start(own_loads)
        lax.fori_loop(0, images, store, 0)
        wait(own_loads)
        start(own_stores)
        me = lax.axis_index("dp")
        vec, tok = refs.vec, refs.tok
        across = pltpu.roll(vec[...], ch - me * part, axis=1)
        for k, ref in enumerate((refs.g_gain1, refs.g_shift1, refs.g_gain2, refs.g_shift2, refs.g_out_bias)):
            ref[...] = across[k, 0:part]
        refs.g_tok_out_bias[...] = vec[5, 0:patch]
        per_row = ch // hidden_part
        row = vec[pl.ds(6 + me // per_row, 1), :]
        refs.g_chan_in_bias[...] = pltpu.roll(row, ch - lax.rem(me, per_row) * hidden_part, axis=1)[0, 0:hidden_part]
        refs.g_tok_out[...] = tok[1, 0:tok_part, 0:patch]
        refs.g_tok_in[...] = tok[0, 0:tok_part, 0:patch]
        refs.g_tok_in_bias[...] = jnp.transpose(tok[0])[patch, 0:tok_part]
        wait(own_stores)
        lax.fori_loop(0, images, finish, 0)

    inputs = dict(
        raw_mixed=(raw.mixed, ANYWHERE), raw_grad=(raw.grad_patches, ANYWHERE), own=(raw.own_out, ANYWHERE),
        tok=(raw.tok_fin, VMEM), vec=(raw.vec_out, VMEM),
    )
    vector, big = ((part,), F32), ((part, sz.hidden), F32)
    outputs = dict(
        mixed=(((images, patch, ch), BF16), ANYWHERE), grad_patches=(((images, patch, ch), F32), ANYWHERE),
        g_gain1=(vector, VMEM), g_shift1=(vector, VMEM), g_tok_in=(((tok_part, patch), F32), VMEM),
        g_tok_in_bias=(((tok_part,), F32), VMEM), g_tok_out=(((tok_part, patch), F32), VMEM),
        g_tok_out_bias=(((patch,), F32), VMEM), g_gain2=(vector, VMEM), g_shift2=(vector, VMEM),
        g_chan_in=(big, ANYWHERE), g_chan_in_bias=(((hidden_part,), F32), VMEM), g_chan_out=(big, ANYWHERE),
        g_out_bias=(vector, VMEM),
    )
    dma = pltpu.SemaphoreType.DMA
    scratch = dict(
        tmp_mixed=pltpu.VMEM((images, patch, ch), BF16), tmp_grad=pltpu.VMEM((images, patch, ch), BF16),
        tmp_wide=pltpu.VMEM((images, patch, ch), F32), tmp_own=pltpu.VMEM((2, part, sz.hidden), F32),
        load_sem=dma((2, images)), store_sem=dma((2, images)), own_sem=dma((3,)),
    )
    results = call_kernel(kernel, inputs, outputs, scratch, 62)
    results.g_tok_in, results.g_chan_out = results.g_tok_in.T, results.g_chan_out.T
    return tuple(vars(results).values())


def local(sz, counts, patches, grad_out, weights, tok_out_bias, params):
    def kernel(refs):
        layer = Layer(sz, refs)
        gw_slot, gw_sem = refs.gw_slot, refs.gw_sem

        def columns(j):
            return pl.ds(pl.multiple_of(j * sz.width, sz.width), sz.width)

        def weight_loads(j, slot):
            return [
                pltpu.make_async_copy(refs.weights.at[m, :, columns(j)], layer.w_slot.at[slot, m], layer.w_sem.at[slot, m])
                for m in range(2)
            ]

        def grad_stores(j, m):
            return [pltpu.make_async_copy(gw_slot.at[m], refs.g_weights.at[m, :, columns(j)], gw_sem.at[m])]

        layer.begin()
        start(weight_loads(0, 0))
        layer.clear()
        lax.fori_loop(0, sz.pairs, layer.mask_pair, 0)
        lax.fori_loop(0, sz.pairs, layer.norm_pair, 0)

        def forward_step(pair, carry):
            layer.token_forward(pair)
            return carry

        lax.fori_loop(0, sz.pairs, forward_step, 0)
        layer.token_forward_end()

        start(layer.back_copies(0, 0))

        def block_step(late, j, carry):
            slot = lax.rem(j, 2)
            wait(weight_loads(j, slot))

            @pl.when(j + 1 < sz.blocks)
            def _():
                start(weight_loads(j + 1, 1 - slot))

            def chunk(r, carry):
                layer.row_chunk(j, slot, r, late)
                return carry

            lax.fori_loop(0, sz.chunks, chunk, 0)
            for m in range(2):

                @pl.when(j >= 1)
                def _():
                    wait(grad_stores(j - 1, m))

                gw_slot[m] = layer.weight_grad(m, slot)
                start(grad_stores(j, m))
            return carry

        lax.fori_loop(0, sz.blocks - 2, functools.partial(block_step, False), 0)
        lax.fori_loop(sz.blocks - 2, sz.blocks, functools.partial(block_step, True), 0)
        for m in range(2):
            wait(grad_stores(sz.blocks - 1, m))

        def backward_step(pair, carry):
            layer.token_backward(pair)
            return carry

        lax.fori_loop(0, sz.pairs, backward_step, 0)
        layer.token_backward_end()

        def output(pair, carry):
            layer.finish_output(pair)
            return carry

        lax.fori_loop(0, sz.pairs, output, 0)
        layer.finish_output_end()

    inputs = dict(
        counts=(counts, SMEM), patches=(patches, ANYWHERE), grad_out=(grad_out, ANYWHERE), weights=(weights, ANYWHERE),
        tok_out_bias=(tok_out_bias, VMEM),
    )
    inputs.update({name: (params[name], VMEM) for name in layer_params(sz)})
    outputs = {name: (of, ANYWHERE) for name, of in layer_results(sz).items()}
    outputs.update(g_weights=(((2, sz.channels, sz.hidden), F32), ANYWHERE))
    outputs.update({name: (of, VMEM) for name, of in layer_sums(sz).items()})
    scratch = layer_scratch(sz, (sz.channels,))
    scratch.update(gw_slot=pltpu.VMEM((2, sz.channels, sz.width), F32), gw_sem=pltpu.SemaphoreType.DMA((2,)))
    return call_kernel(kernel, inputs, outputs, scratch, 62)


def on_device(
    patches, image_counts, grad_out,
    ln1_gain, ln1_bias, w_token_in, b_token_in, w_token_out, b_token_out,
    ln2_gain, ln2_bias, w_chan_in, b_chan_in, w_chan_out, b_chan_out,
):
    images, patch, ch = patches.shape
    token_part, hidden_part, part = b_token_in.shape[0], b_chan_in.shape[0], ln1_gain.shape[0]
    n_dp = lax.axis_size("dp")
    hidden = w_chan_in.shape[1]
    sz = Sizes(images, patch, ch, token_part * n_dp, hidden, 512, images * (-(-patch // 8) * 8) // 3)
    pad = sz.padded
    vectors = (ln1_gain, ln1_bias, ln2_gain, ln2_bias, b_chan_out)

    def own(vector, length):
        return lax.dynamic_slice_in_dim(vector, lax.axis_index("dp") * length, length)

    if n_dp == 16 and sz.pairs == 6 and part % 16 == 0 and token_part % 8 == 0 and part % token_part == 0:
        res = networked(
            sz, image_counts, patches, grad_out, ln1_gain=ln1_gain, ln1_bias=ln1_bias, w_token_in=w_token_in.T,
            b_token_in=b_token_in, w_token_out=w_token_out, b_token_out=b_token_out, ln2_gain=ln2_gain,
            ln2_bias=ln2_bias, w_chan_in=w_chan_in, b_chan_in=b_chan_in, w_chan_out=w_chan_out.T,
            b_chan_out=b_chan_out,
        )
        return hand_out(sz, res, token_part, hidden_part)
    else:
        tok_out_bias = jnp.pad(b_token_out.astype(F32), (0, pad - patch))[:, None]
        weights = lax.all_gather(jnp.stack([w_chan_in, w_chan_out.T]), "dp", axis=1, tiled=True)
        tokens = lax.all_gather(jnp.stack([w_token_in.T, w_token_out]), "dp", axis=1, tiled=True)
        tokens = jnp.pad(tokens, ((0, 0), (0, 0), (0, pad - patch)))
        every = lax.all_gather(jnp.concatenate(vectors + (b_token_in, b_chan_in)), "dp", axis=0)
        whole = [every[:, k * part : (k + 1) * part].reshape(1, ch).astype(F32) for k in range(5)]
        tok_bias = every[:, 5 * part : 5 * part + token_part].reshape(-1)
        gain1, shift1, gain2, shift2, out_bias = whole
        params = dict(
            gain1=gain1, shift1=shift1, gain2=gain2, shift2=shift2, out_bias=out_bias,
            tok_in_t=tokens[0].at[:, patch].set(tok_bias), tok_in=tokens[0].T,
            tok_out_t=tokens[1].T, tok_out=tokens[1],
            chan_in_bias=every[:, 5 * part + token_part :].reshape(sz.blocks, 1, sz.width).astype(F32),
        )
        res = local(sz, image_counts, patches, grad_out, weights, tok_out_bias, params)
        g_weights = lax.psum_scatter(res.g_weights.astype(BF16), "dp", scatter_dimension=1, tiled=True)
        g_weights = lax.psum(g_weights, "outer").astype(F32)
        g_tokens = lax.psum(lax.psum_scatter(res.g_tok, "dp", scatter_dimension=1, tiled=True), "outer")
        sums = [jnp.sum(v, axis=0) for v in (res.g_gain1, res.g_shift1, res.g_gain2, res.g_shift2, res.g_out_bias)]
        sums += [jnp.sum(res.g_chan_in_bias, axis=1).reshape(-1), res.g_tok_out_bias[:patch, 0]]
        sums = lax.psum(tuple(sums), ("dp", "outer"))
        g_vec = [own(vector, part) for vector in sums[:5]]
        g_chan_bias, g_tok_out_bias = own(sums[5], hidden_part), sums[6]

    return (
        res.mixed, res.grad_patches.astype(F32),
        g_vec[0], g_vec[1], g_tokens[0, :, :patch].T, g_tokens[0, :, patch], g_tokens[1, :, :patch], g_tok_out_bias,
        g_vec[2], g_vec[3], g_weights[0], g_chan_bias, g_weights[1].T, g_vec[4],
    )


def solution(mesh):
    slots = P(("dp", "outer"), None, None)
    return jax.shard_map(
        on_device,
        mesh=mesh,
        in_specs=(
            slots, P(("dp", "outer")), slots, P("dp"), P("dp"), P(None, "dp"), P("dp"), P("dp", None), P(),
            P("dp"), P("dp"), P("dp", None), P("dp"), P(None, "dp"), P("dp"),
        ),
        out_specs=(
            slots, slots, P("dp"), P("dp"), P(None, "dp"), P("dp"), P("dp", None), P(),
            P("dp"), P("dp"), P("dp", None), P("dp"), P(None, "dp"), P("dp"),
        ),
        check_vma=False,
    )
```

```python
import functools
import types

import jax
import jax.numpy as jnp
from jax import lax
from jax.experimental import pallas as pl
from jax.experimental.pallas import tpu as pltpu
from jax.sharding import PartitionSpec as P

EPS = 1e-06
F32 = jnp.float32
BF16 = jnp.bfloat16
NN = (((1,), (0,)), ((), ()))
NT = (((1,), (1,)), ((), ()))
TN = (((0,), (0,)), ((), ()))
MESH = pl.DeviceIdType.MESH
ROOT = 0.7978845608028654
CUBE = 0.044715 * ROOT


def dot(left, right, dims):
    return lax.dot_general(left, right, dims, preferred_element_type=F32)


def gelu_both(value):
    square = value * value
    half = 0.5 + 0.5 * jnp.tanh(value * (ROOT + CUBE * square))
    slope = half + (half - half * half) * (value * (2 * ROOT + 6 * CUBE * square))
    return value * half, slope


def fold(values):
    return jnp.sum(values.reshape(values.shape[0] // 8, 8, values.shape[1]), axis=0)


def lane_mean(values):
    return jnp.mean(values, axis=-1, keepdims=True)


def standardize(values):
    centered = values - lane_mean(values)
    scale = lax.rsqrt(lane_mean(centered * centered) + EPS)
    return centered * scale, scale


def pad_rows(values, rows):
    extra = rows - values.shape[0]
    if extra == 0:
        return values
    return jnp.concatenate([values, jnp.zeros((extra, values.shape[1]), values.dtype)], axis=0)


class Sizes:
    def __init__(self, images, patches, channels, token_hidden, hidden, width, rows):
        self.images, self.patches, self.channels = images, patches, channels
        self.token_hidden, self.hidden, self.width = token_hidden, hidden, width
        self.padded = -(-patches // 8) * 8
        self.flat = images * self.padded
        self.blocks = hidden // width
        self.rows = rows
        self.chunks = self.flat // rows
        self.pairs = images // 2
        self.lanes = -(-self.padded // 128) * 128


def start(copies):
    for copy in copies:
        copy.start()


def wait(copies):
    for copy in copies:
        copy.wait()


class Place:
    def __init__(self):
        me, c = lax.axis_index("dp"), lax.axis_index("outer")
        z = me // 4
        yx = me - 4 * z
        y = yx // 2
        x = yx - 2 * y
        step_x, step_y = 1 - 2 * x, 2 * (1 - 2 * y)
        self.c, self.z, self.yx = c, z, yx
        self.yx_a = yx + (1 - c) * step_x + c * step_y
        self.yx_b = yx + c * step_x + (1 - c) * step_y
        self.yx_ab = yx + step_x + step_y
        self.sibling = (me, 1 - c)
        self.peer_a, self.peer_b = (4 * z + self.yx_a, c), (4 * z + self.yx_b, c)
        self.z_of = [lax.rem(z + k, 4) for k in range(4)]
        self.peer_z = [(4 * self.z_of[k] + yx, c) for k in range(4)]
        self.peers_xy = [self.peer_a, self.peer_b, (4 * z + self.yx_ab, c)]
        self.yx_xy = [self.yx_a, self.yx_b, self.yx_ab]

    def greet(self):
        barrier = pltpu.get_barrier_semaphore()
        for peer in [self.sibling] + self.peers_xy + self.peer_z[1:]:
            pl.semaphore_signal(barrier, inc=1, device_id=peer, device_id_type=MESH)

    def meet(self):
        pl.semaphore_wait(pltpu.get_barrier_semaphore(), 7)


def remote(source, target, sems, index, peer):
    return pltpu.make_async_remote_copy(
        src_ref=source, dst_ref=target, send_sem=sems[0].at[index], recv_sem=sems[1].at[index],
        device_id=peer, device_id_type=MESH,
    )


class Gather:
    def __init__(self, place, own, view, sems, base):
        self.place, self.own, self.view, self.sems, self.base = place, own, view, sems, base

    def send(self, position, index, peer):
        ref = self.view(self.place.c, slice(None), position)
        return remote(ref, ref, self.sems, self.base + index, peer)

    @property
    def along_z(self):
        place = self.place
        target = self.view(place.c, place.z, place.yx)
        return [remote(self.own, target, self.sems, self.base + k - 1, place.peer_z[k]) for k in (1, 2, 3)]

    @property
    def along_a(self):
        return [self.send(self.place.yx, 3, self.place.peer_a)]

    @property
    def along_b(self):
        place = self.place
        return [self.send(place.yx, 4, place.peer_b), self.send(place.yx_a, 5, place.peer_b)]

    @property
    def along_xy(self):
        place = self.place
        return [self.send(place.yx, 3 + k, place.peers_xy[k]) for k in range(3)]

    @property
    def swap(self):
        return [self.send(slice(None), 6, self.place.sibling)]

    def to_xy(self):
        wait(self.along_z)
        start(self.along_xy)

    def xy_to_sibling(self):
        wait(self.along_xy)
        start(self.swap)

    def to_a(self):
        wait(self.along_z)
        start(self.along_a)

    def to_b(self):
        wait(self.along_a)
        start(self.along_b)

    def to_sibling(self):
        wait(self.along_b)
        start(self.swap)


class Reduce:
    def __init__(self, place, refs, own_out, sems, base, slot):
        (self.mine, csend, crecv, self.send1, self.keep1, recv1, self.send2, self.keep2, recv2,
         self.send3, self.keep3, recv3) = refs
        self.place, self.own_out, self.csend, self.sems, self.base = place, own_out, csend, sems, base
        self.crecv, self.recv1, self.recv2, self.recv3 = crecv.at[slot], recv1.at[slot], recv2.at[slot], recv3.at[slot]

    def send(self, source, target, index, peer):
        return remote(source, target, self.sems, self.base + index, peer)

    @property
    def swap(self):
        return [self.send(self.csend, self.crecv, 0, self.place.sibling)]

    @property
    def along_b(self):
        return [self.send(self.send1, self.recv1, 1, self.place.peer_b)]

    @property
    def along_a(self):
        return [self.send(self.send2, self.recv2, 2, self.place.peer_a)]

    @property
    def along_z(self):
        place = self.place
        return [
            self.send(self.send3.at[place.z_of[k]], self.recv3.at[k - 1], 2 + k, place.peer_z[k]) for k in (1, 2, 3)
        ]

    @property
    def finish(self):
        return [self.send(self.own_out, self.own_out, 6, self.place.sibling)]

    def to_b(self):
        wait(self.swap)
        place = self.place

        def step(z, carry):
            for q, (kept, sent) in enumerate(((place.yx, place.yx_b), (place.yx_a, place.yx_ab))):
                self.keep1[z, q] = (self.mine[z, kept].astype(F32) + self.crecv[z, kept].astype(F32)).astype(BF16)
                self.send1[z, q] = (self.mine[z, sent].astype(F32) + self.crecv[z, sent].astype(F32)).astype(BF16)
            return carry

        lax.fori_loop(0, 4, step, 0)
        start(self.along_b)

    def to_a(self):
        wait(self.along_b)

        def step(z, carry):
            self.keep2[z] = self.keep1[z, 0].astype(F32) + self.recv1[z, 0].astype(F32)
            self.send2[z] = (self.keep1[z, 1].astype(F32) + self.recv1[z, 1].astype(F32)).astype(BF16)
            return carry

        lax.fori_loop(0, 4, step, 0)
        start(self.along_a)

    def to_z(self):
        wait(self.along_a)

        def step(z, carry):
            self.send3[z] = (self.keep2[z] + self.recv2[z].astype(F32)).astype(BF16)
            return carry

        lax.fori_loop(0, 4, step, 0)
        z = self.place.z
        self.keep3[...] = self.keep2[z] + self.recv2[z].astype(F32)
        start(self.along_z)

    def to_owner(self):
        wait(self.along_z)
        total = self.keep3[...]
        for k in range(3):
            total += self.recv3[k].astype(F32)
        self.own_out[...] = total
        start(self.finish)


class SmallReduce:
    def __init__(self, place, refs, own_out, sems):
        self.mine, self.csend, self.crecv, self.send1, self.keep1, self.recv1, self.send3, self.keep3, self.recv3 = refs
        self.place, self.own_out, self.sems = place, own_out, sems

    def send(self, source, target, index, peer):
        return remote(source, target, self.sems, index, peer)

    @property
    def swap(self):
        return [self.send(self.csend, self.crecv, 0, self.place.sibling)]

    @property
    def along_xy(self):
        place = self.place
        return [self.send(self.send1.at[k], self.recv1.at[k], 1 + k, place.peers_xy[k]) for k in range(3)]

    @property
    def along_z(self):
        place = self.place
        return [
            self.send(self.send3.at[place.z_of[k]], self.recv3.at[k - 1], 3 + k, place.peer_z[k]) for k in (1, 2, 3)
        ]

    @property
    def finish(self):
        return [self.send(self.own_out, self.own_out, 7, self.place.sibling)]

    def to_xy(self):
        wait(self.swap)
        place = self.place
        for k in range(3):
            at = place.yx_xy[k]
            self.send1[k] = (self.mine[:, at] + self.crecv[:, at].astype(F32)).astype(BF16)
        start(self.along_xy)
        self.keep1[...] = self.mine[:, place.yx] + self.crecv[:, place.yx].astype(F32)

    def to_z(self):
        wait(self.along_xy)
        total = self.keep1[...]
        for k in range(3):
            total += self.recv1[k].astype(F32)
        self.send3[...] = total.astype(BF16)
        start(self.along_z)
        self.keep1[...] = total
        self.keep3[...] = self.keep1[self.place.z]

    def to_owner(self):
        wait(self.along_z)
        total = self.keep3[...]
        for k in range(3):
            total += self.recv3[k].astype(F32)
        self.own_out[...] = total
        start(self.finish)


def small_reduce_scratch(part, width):
    return [
        pltpu.VMEM((4, 4, part, width), F32),
        pltpu.VMEM((4, 4, part, width), BF16), pltpu.VMEM((4, 4, part, width), BF16),
        pltpu.VMEM((3, 4, part, width), BF16), pltpu.VMEM((4, part, width), F32),
        pltpu.VMEM((3, 4, part, width), BF16),
        pltpu.VMEM((4, part, width), BF16), pltpu.VMEM((part, width), F32),
        pltpu.VMEM((3, part, width), BF16),
    ]


def reduce_scratch(part, width, slots):
    return [
        pltpu.VMEM((4, 4, part, width), BF16),
        pltpu.VMEM((4, 4, part, width), BF16), pltpu.VMEM((slots, 4, 4, part, width), BF16),
        pltpu.VMEM((4, 2, part, width), BF16), pltpu.VMEM((4, 2, part, width), BF16),
        pltpu.VMEM((slots, 4, 2, part, width), BF16),
        pltpu.VMEM((4, part, width), BF16), pltpu.VMEM((4, part, width), F32),
        pltpu.VMEM((slots, 4, part, width), BF16),
        pltpu.VMEM((4, part, width), BF16), pltpu.VMEM((part, width), F32),
        pltpu.VMEM((slots, 3, part, width), BF16),
    ]


class Layer:
    def __init__(self, sz, refs):
        self.sz = sz
        self.__dict__.update(vars(refs))

    def load_copies(self, pair, slot):
        return [
            pltpu.make_async_copy(self.patches.at[pair * 2 + k], self.x_slot.at[slot, k], self.load_sem.at[slot, k])
            for k in range(2)
        ]

    def next_images(self, pair):
        slot = lax.rem(pair, 2)
        following = jnp.where(pair + 1 < self.sz.pairs, pair + 1, 0)
        start(self.load_copies(following, 1 - slot))
        wait(self.load_copies(pair, slot))

    def image_of(self, pair, k):
        return pad_rows(self.x_slot[lax.rem(pair, 2), k].astype(F32), self.sz.padded)

    def cotangent_copies(self, pair, slot):
        return [
            pltpu.make_async_copy(self.grad_out.at[pair * 2 + k], self.mixed_slot.at[slot, k], self.out_sem.at[slot, k, 0])
            for k in range(2)
        ]

    def keep_copies(self, pair, slot, k):
        i = pair * 2 + k
        return [
            pltpu.make_async_copy(self.act_slot.at[slot, k], self.kept_act.at[i], self.act_sem.at[slot, k, 0]),
            pltpu.make_async_copy(self.slope_slot.at[slot, k], self.kept_slope.at[i], self.act_sem.at[slot, k, 1]),
        ]

    def back_copies(self, pair, slot):
        copies = []
        for k in range(2):
            i = pair * 2 + k
            copies += [
                pltpu.make_async_copy(self.kept_act.at[i], self.act_slot.at[slot, k], self.act_sem.at[slot, k, 0]),
                pltpu.make_async_copy(self.kept_slope.at[i], self.slope_slot.at[slot, k], self.act_sem.at[slot, k, 1]),
            ]
        return copies

    def result_copies(self, pair, slot, k):
        i = pair * 2 + k
        return [
            pltpu.make_async_copy(self.gp_slot.at[slot, k], self.grad_patches.at[i], self.out_sem.at[slot, k, 1]),
        ]

    def begin(self):
        start(self.load_copies(0, 0))
        start(self.cotangent_copies(0, 0))

    def clear(self):
        for ref in (self.g_gain1, self.g_shift1, self.g_gain2, self.g_shift2, self.g_out_bias, self.g_tok_out_bias,
                    self.g_tok, self.g_chan_in_bias):
            ref[...] = jnp.zeros_like(ref)

    def kept(self, i):
        return jnp.where(i < self.counts[0], 1.0, 0.0)

    def both(self, pair):
        return pl.ds(pl.multiple_of(pair * 2 * self.sz.padded, 16), 2 * self.sz.padded)

    def image(self, i):
        return pl.ds(pl.multiple_of(i * self.sz.padded, 8), self.sz.padded)

    def mask_pair(self, pair, carry):
        sz, slot = self.sz, lax.rem(pair, 2)

        @pl.when(pair + 1 < sz.pairs)
        def _():
            start(self.cotangent_copies(pair + 1, 1 - slot))

        wait(self.cotangent_copies(pair, slot))
        cotangent = jnp.concatenate(
            [pad_rows(self.mixed_slot[slot, k].astype(F32), sz.padded) * self.kept(pair * 2 + k) for k in range(2)],
            axis=0,
        )
        self.lhs[1, self.both(pair), :] = cotangent.astype(BF16)
        self.g_out_bias[...] += fold(cotangent)
        return carry

    def norm_pair(self, pair, carry):
        self.next_images(pair)
        for k in range(2):
            xhat, _ = standardize(self.image_of(pair, k))
            self.total_din[self.image(pair * 2 + k), :] = xhat
        return carry

    def token_input(self, xhat):
        patch = self.sz.patches
        value = xhat * self.gain1[...] + self.shift1[...]
        whole = patch // 8 * 8
        rest = value[whole:]
        row = lax.broadcasted_iota(jnp.int32, rest.shape, 0) + whole
        rest = jnp.where(row < patch, rest, jnp.where(row == patch, 1.0, 0.0))
        return jnp.concatenate([value[:whole], rest], axis=0).astype(BF16)

    def token_forward(self, pair):
        sz, slot = self.sz, lax.rem(pair, 2)

        @pl.when(pair >= 2)
        def _():
            for k in range(2):
                wait(self.keep_copies(pair - 2, slot, k))

        self.next_images(pair)
        both = self.both(pair)
        residuals = []
        for k in range(2):
            i = pair * 2 + k
            token_in = self.token_input(self.total_din[self.image(i), :])
            act, slope = gelu_both(dot(self.tok_in_t[...], token_in, NN))
            act = act.astype(BF16)
            self.act_slot[slot, k] = act
            self.slope_slot[slot, k] = slope.astype(BF16)
            residuals.append(self.image_of(pair, k) + dot(self.tok_out_t[...], act, NN) + self.tok_out_bias[...])
        residual = jnp.concatenate(residuals, axis=0)
        hat, scale = standardize(residual)
        self.lhs[0, both, :] = (hat * self.gain2[...] + self.shift2[...]).astype(BF16)
        self.xhat2[both, :] = hat.astype(BF16)
        lane = lax.broadcasted_iota(jnp.int32, self.scale2.shape, 1)
        self.scale2[...] = jnp.where(lane == pair, scale, self.scale2[...])
        self.total_out[both, :] = residual + self.out_bias[...]
        self.total_din[both, :] = jnp.zeros((2 * sz.padded, sz.channels), F32)
        for k in range(2):
            start(self.keep_copies(pair, slot, k))

    def token_forward_end(self):
        for pair in range(max(0, self.sz.pairs - 2), self.sz.pairs):
            for k in range(2):
                wait(self.keep_copies(pair, pair % 2, k))

    def weights_of(self, slot, matrix):
        return self.w_slot[slot, matrix].reshape(self.sz.channels, self.sz.width)

    def row_chunk(self, j, slot, r, late):
        sz = self.sz
        rows = pl.ds(pl.multiple_of(r * sz.rows, 16), sz.rows)
        w_in, w_out = self.weights_of(slot, 0), self.weights_of(slot, 1)
        pre = dot(self.lhs[0, rows, :], w_in, NN) + self.chan_in_bias[j]
        d_act = dot(self.lhs[1, rows, :], w_out, NN)
        act, slope = gelu_both(pre)
        act = act.astype(BF16)
        d_pre = d_act * slope
        self.g_chan_in_bias[j] += fold(d_pre)
        d_pre = d_pre.astype(BF16)
        self.rhs[1 + slot, rows, :] = act
        self.rhs[0, rows, :] = d_pre
        if not late:
            self.total_out[rows, :] += dot(act, w_out, NT)
        self.total_din[rows, :] += dot(d_pre, w_in, NT)

    def weight_grad(self, matrix, slot):
        return dot(self.lhs[matrix], self.rhs[matrix * (1 + slot)], TN)

    def mixed_copies(self, pair, slot):
        return [
            pltpu.make_async_copy(self.mixed_slot.at[slot, k], self.mixed.at[pair * 2 + k], self.out_sem.at[slot, k, 0])
            for k in range(2)
        ]

    def finish_output(self, pair):
        sz, slot = self.sz, lax.rem(pair, 2)

        @pl.when(pair >= 2)
        def _():
            wait(self.mixed_copies(pair - 2, slot))

        both = self.both(pair)
        total = self.total_out[both, :]
        for late in range(2):
            total += dot(self.rhs[1 + late, both, :], self.weights_of(late, 1), NT)
        for k in range(2):
            layer = total[k * sz.padded : k * sz.padded + sz.padded] * self.kept(pair * 2 + k)
            self.mixed_slot[slot, k] = layer[: sz.patches].astype(BF16)
        start(self.mixed_copies(pair, slot))

    def finish_output_end(self):
        for pair in range(self.sz.pairs - 2, self.sz.pairs):
            wait(self.mixed_copies(pair, pair % 2))

    def token_backward(self, pair):
        sz, slot = self.sz, lax.rem(pair, 2)
        pad = sz.padded

        @pl.when(pair + 1 < sz.pairs)
        def _():
            start(self.back_copies(pair + 1, 1 - slot))

        @pl.when(pair >= 2)
        def _():
            for k in range(2):
                wait(self.result_copies(pair - 2, slot, k))

        self.next_images(pair)
        both = self.both(pair)
        d_in = self.total_din[both, :]
        hat = self.xhat2[both, :].astype(F32)
        self.g_gain2[...] += fold(d_in * hat)
        self.g_shift2[...] += fold(d_in)
        e = d_in * self.gain2[...]
        lane = lax.broadcasted_iota(jnp.int32, self.scale2.shape, 1)
        scale2 = jnp.sum(jnp.where(lane == pair, self.scale2[...], 0.0), axis=-1, keepdims=True)
        d_residual = self.lhs[1, both, :].astype(F32) + scale2 * (
            e - lane_mean(e) - hat * lane_mean(e * hat)
        )
        rounded = d_residual.astype(BF16).astype(F32)
        wait(self.back_copies(pair, slot))
        for k in range(2):
            i = pair * 2 + k
            part = slice(k * pad, (k + 1) * pad)
            d_token_out = rounded[part].astype(BF16)
            self.g_tok[1] += dot(self.act_slot[slot, k], d_token_out, NT)
            self.g_tok_out_bias[...] += jnp.sum(rounded[part], axis=-1, keepdims=True)
            d_pre = dot(self.tok_out[...], d_token_out, NN) * self.slope_slot[slot, k].astype(F32)
            d_pre = d_pre.astype(BF16)
            hat1, scale1 = standardize(self.image_of(pair, k))
            self.g_tok[0] += dot(d_pre, self.token_input(hat1), NT)
            d_token_in = dot(self.tok_in[...], d_pre, NN)
            self.g_gain1[...] += fold(d_token_in * hat1)
            self.g_shift1[...] += fold(d_token_in)
            f = d_token_in * self.gain1[...]
            result = d_residual[part] + scale1 * (f - lane_mean(f) - hat1 * lane_mean(f * hat1))
            self.gp_slot[slot, k] = result[: sz.patches].astype(BF16)
            start(self.result_copies(pair, slot, k))

    def token_backward_end(self):
        wait(self.load_copies(0, self.sz.pairs % 2))
        for pair in range(max(0, self.sz.pairs - 2), self.sz.pairs):
            for k in range(2):
                wait(self.result_copies(pair, pair % 2, k))


def layer_scratch(sz, weight_shape):
    images, patch, ch = sz.images, sz.patches, sz.channels
    return dict(
        x_slot=pltpu.VMEM((2, 2, patch, ch), BF16),
        lhs=pltpu.VMEM((2, sz.flat, ch), BF16), xhat2=pltpu.VMEM((sz.flat, ch), BF16),
        scale2=pltpu.VMEM((2 * sz.padded, 128), F32),
        total_out=pltpu.VMEM((sz.flat, ch), F32), total_din=pltpu.VMEM((sz.flat, ch), F32),
        act_slot=pltpu.VMEM((2, 2, sz.token_hidden, ch), BF16),
        slope_slot=pltpu.VMEM((2, 2, sz.token_hidden, ch), BF16),
        rhs=pltpu.VMEM((3, sz.flat, sz.width), BF16),
        w_slot=pltpu.VMEM((2, 2) + weight_shape + (sz.width,), BF16),
        mixed_slot=pltpu.VMEM((2, 2, patch, ch), BF16), gp_slot=pltpu.VMEM((2, 2, patch, ch), BF16),
        load_sem=pltpu.SemaphoreType.DMA((2, 2)), act_sem=pltpu.SemaphoreType.DMA((2, 2, 2)),
        w_sem=pltpu.SemaphoreType.DMA((2, 2)), out_sem=pltpu.SemaphoreType.DMA((2, 2, 2)),
    )


def layer_sums(sz):
    ch = sz.channels
    return dict(
        g_gain1=((8, ch), F32), g_shift1=((8, ch), F32), g_gain2=((8, ch), F32), g_shift2=((8, ch), F32),
        g_out_bias=((8, ch), F32), g_tok_out_bias=((sz.padded, 1), F32),
        g_tok=((2, sz.token_hidden, sz.padded), F32), g_chan_in_bias=((sz.blocks, 8, sz.width), F32),
    )


def layer_params(sz):
    ch, pad, th = sz.channels, sz.padded, sz.token_hidden
    return dict(
        gain1=((1, ch), F32), shift1=((1, ch), F32), gain2=((1, ch), F32), shift2=((1, ch), F32),
        out_bias=((1, ch), F32), tok_in_t=((th, pad), BF16), tok_in=((pad, th), BF16),
        tok_out_t=((pad, th), BF16), tok_out=((th, pad), BF16), chan_in_bias=((sz.blocks, 1, sz.width), F32),
    )


def layer_results(sz):
    return dict(
        mixed=((sz.images, sz.patches, sz.channels), BF16),
        grad_patches=((sz.images, sz.patches, sz.channels), BF16),
        kept_act=((sz.images, sz.token_hidden, sz.channels), BF16),
        kept_slope=((sz.images, sz.token_hidden, sz.channels), BF16),
    )


def call_kernel(kernel, inputs, outputs, scratch, vmem_mib, **params):
    names = list(inputs) + list(outputs) + list(scratch)

    def body(*refs):
        kernel(types.SimpleNamespace(**dict(zip(names, refs))))

    results = pl.pallas_call(
        body,
        out_shape=[jax.ShapeDtypeStruct(*of) for of, _ in outputs.values()],
        in_specs=[spec for _, spec in inputs.values()],
        out_specs=[spec for _, spec in outputs.values()],
        scratch_shapes=list(scratch.values()),
        compiler_params=pltpu.CompilerParams(vmem_limit_bytes=vmem_mib * 2**20, **params),
    )(*[array for array, _ in inputs.values()])
    return types.SimpleNamespace(**dict(zip(outputs, results)))


ANYWHERE = pl.BlockSpec(memory_space=pl.ANY)
VMEM = pl.BlockSpec(memory_space=pltpu.VMEM)
SMEM = pl.BlockSpec(memory_space=pltpu.SMEM)


def networked(sz, counts, patches, grad_out, **params):
    part = sz.channels // 16
    tok_part = sz.token_hidden // 16
    pack_rows = -(-(tok_part + 1) // 16) * 16
    blocks, width = sz.blocks, sz.width
    n_gather, n_reduce = blocks + 1, blocks

    def kernel(refs):
        place = Place()
        layer = Layer(sz, refs)
        gathered, pack_all = refs.gathered, refs.pack_all
        gather_sems = (refs.gather_send, refs.gather_recv)
        reduce_sems = (refs.reduce_send, refs.reduce_recv)
        vector_sems = (refs.vector_send, refs.vector_recv)
        own_out, tok_fin = refs.own_out, refs.tok_fin
        c = place.c
        chan_refs = [getattr(refs, "c%d" % k) for k in range(12)]
        tok_refs = [getattr(refs, "t%d" % k) for k in range(9)]

        def columns(j):
            return pl.ds(pl.multiple_of(j * width, width), width)

        def gather(j):
            cols = columns(j)

            def view(matrix, z, yx):
                return gathered.at[matrix, z, yx, :, cols]

            return Gather(place, refs.own_weight.at[:, cols], view, gather_sems, j * 7)

        def pack_view(matrix, z, yx):
            return pack_all.at[matrix, z, yx]

        pack = Gather(place, refs.pack_own, pack_view, gather_sems, blocks * 7)

        def reduce(j):
            return Reduce(place, chan_refs, own_out.at[c, :, columns(j)], reduce_sems, j * 7, lax.rem(j, 2))

        tok_reduce = SmallReduce(place, tok_refs, tok_fin.at[c], (refs.tok_send, refs.tok_recv))

        def own_load(source):
            return [pltpu.make_async_copy(source, refs.own_weight, refs.own_sem.at[2])]

        own_copies = [
            pltpu.make_async_copy(refs.own_weight, gathered.at[c, place.z, place.yx], refs.own_sem.at[0]),
            pltpu.make_async_copy(refs.pack_own, pack_all.at[c, place.z, place.yx], refs.own_sem.at[1]),
        ]

        def weight_loads(j, slot):
            return [
                pltpu.make_async_copy(
                    gathered.at[m, :, :, :, columns(j)], layer.w_slot.at[slot, m], layer.w_sem.at[slot, m]
                )
                for m in range(2)
            ]

        place.greet()

        @pl.when(c == 0)
        def _():
            start(own_load(refs.p_w_chan_in))

        @pl.when(c == 1)
        def _():
            start(own_load(refs.p_w_chan_out))

        layer.begin()
        make_pack(sz, c, refs)
        place.meet()
        start(pack.along_z)
        wait(own_load(refs.p_w_chan_in))
        start(own_copies)
        start(gather(0).along_z)
        layer.clear()
        lax.fori_loop(0, sz.pairs, layer.mask_pair, 0)
        wait(own_copies)
        pack.to_xy()
        lax.fori_loop(0, sz.pairs // 2, layer.norm_pair, 0)
        gather(0).to_a()
        start(gather(1).along_z)
        lax.fori_loop(sz.pairs // 2, sz.pairs, layer.norm_pair, 0)
        pack.xy_to_sibling()
        wait(pack.swap)
        unpack(sz, layer, pack_all, tok_part)
        gather(0).to_b()
        gather(1).to_a()
        start(gather(2).along_z)

        def forward_step(pair, carry):
            layer.token_forward(pair)

            @pl.when(pair == 3)
            def _():
                gather(0).to_sibling()
                gather(1).to_b()
                gather(2).to_a()
                start(gather(3).along_z)

            @pl.when(pair == 5)
            def _():
                wait(gather(0).swap)
                start(weight_loads(0, 0))

            return carry

        lax.fori_loop(0, sz.pairs, forward_step, 0)
        layer.token_forward_end()

        start(layer.back_copies(0, 0))

        def block_step(late, j, carry):
            slot = lax.rem(j, 2)
            wait(weight_loads(j, slot))

            def chunk(r, carry):
                layer.row_chunk(j, slot, r, late)

                @pl.when(r == 0)
                def _():
                    @pl.when(j >= 2)
                    def _():
                        reduce(j - 2).to_a()

                    @pl.when(j >= 1)
                    def _():
                        reduce(j - 1).to_b()

                @pl.when(r == 1)
                def _():
                    @pl.when(j + 1 < blocks)
                    def _():
                        gather(j + 1).to_sibling()

                    @pl.when(j + 2 < blocks)
                    def _():
                        gather(j + 2).to_b()

                    @pl.when(j + 3 < blocks)
                    def _():
                        gather(j + 3).to_a()

                    @pl.when(j + 4 < blocks)
                    def _():
                        start(gather(j + 4).along_z)

                @pl.when(r == 2)
                def _():
                    @pl.when(j >= 3)
                    def _():
                        reduce(j - 3).to_owner()

                return carry

            lax.fori_loop(0, sz.chunks, chunk, 0)
            mine, csend = chan_refs[0], chan_refs[1]
            csend[...] = layer.weight_grad(1 - c, slot).astype(BF16).reshape(csend.shape)
            start(reduce(j).swap)

            @pl.when(j + 1 < blocks)
            def _():
                wait(gather(j + 1).swap)
                start(weight_loads(j + 1, 1 - slot))

            mine[...] = layer.weight_grad(c, slot).astype(BF16).reshape(mine.shape)

            @pl.when(j >= 2)
            def _():
                reduce(j - 2).to_z()

            return carry

        lax.fori_loop(0, blocks - 2, functools.partial(block_step, False), 0)
        lax.fori_loop(blocks - 2, blocks, functools.partial(block_step, True), 0)

        def backward_step(pair, carry):
            layer.token_backward(pair)

            @pl.when(pair == 0)
            def _():
                reduce(blocks - 2).to_a()
                reduce(blocks - 1).to_b()

            @pl.when(pair == 1)
            def _():
                reduce(blocks - 3).to_owner()

            @pl.when(pair == 2)
            def _():
                reduce(blocks - 2).to_z()

            @pl.when(pair == 4)
            def _():
                reduce(blocks - 2).to_owner()
                reduce(blocks - 1).to_a()

            return carry

        lax.fori_loop(0, sz.pairs, backward_step, 0)

        mine, csend = tok_refs[0], tok_refs[1]

        def packed(matrix):
            value = layer.g_tok[matrix].reshape(16, tok_part, sz.padded)
            return value

        filler = jnp.zeros((16, pack_rows - tok_part, sz.padded), F32)
        for ref, matrix in ((csend, 1 - c), (mine, c)):
            value = jnp.concatenate([packed(matrix), filler], axis=1).astype(ref.dtype)
            ref[:, :, :, 0 : sz.padded] = value.reshape(4, 4, pack_rows, sz.padded)
            ref[:, :, :, sz.padded :] = jnp.zeros((4, 4, pack_rows, sz.lanes - sz.padded), ref.dtype)
            if ref is csend:
                start(tok_reduce.swap)
        vec, vec_in, vec_xy, vec_z = refs.vec, refs.vec_in, refs.vec_xy, refs.vec_z
        vec[...] = jnp.zeros_like(vec)
        for k, ref in enumerate((layer.g_gain1, layer.g_shift1, layer.g_gain2, layer.g_shift2, layer.g_out_bias)):
            vec[k : k + 1, :] = jnp.sum(ref[...], axis=0, keepdims=True)
        column = jnp.broadcast_to(layer.g_tok_out_bias[...], (sz.padded, 128))
        vec[5:6, 0 : sz.padded] = jnp.transpose(column)[0:1]
        flat = [jnp.sum(layer.g_chan_in_bias[j], axis=0, keepdims=True) for j in range(blocks)]
        flat = jnp.concatenate(flat, axis=1)
        for k in range(sz.hidden // sz.channels):
            vec[6 + k : 7 + k, :] = flat[:, k * sz.channels : (k + 1) * sz.channels]

        vector_swap = [remote(vec, vec_in, vector_sems, 0, place.sibling)]
        vector_xy = [remote(vec, vec_xy.at[place.yx], vector_sems, 1 + k, place.peers_xy[k]) for k in range(3)]
        vector_z = [remote(vec, vec_z.at[place.z], vector_sems, 3 + k, place.peer_z[k]) for k in (1, 2, 3)]
        def output(pair, carry):
            layer.finish_output(pair)
            return carry

        start(vector_swap)
        lax.fori_loop(0, 1, output, 0)
        reduce(blocks - 1).to_z()
        tok_reduce.to_xy()
        wait(vector_swap)
        vec[...] += vec_in[...]
        start(vector_xy)
        vec_xy[place.yx] = vec[...]
        lax.fori_loop(1, 4, output, 0)
        tok_reduce.to_z()
        wait(vector_xy)
        vec[...] = (vec_xy[0] + vec_xy[1]) + (vec_xy[2] + vec_xy[3])
        start(vector_z)
        vec_z[place.z] = vec[...]
        lax.fori_loop(4, sz.pairs, output, 0)
        layer.token_backward_end()
        layer.finish_output_end()
        reduce(blocks - 1).to_owner()
        tok_reduce.to_owner()
        wait(vector_z)
        refs.vec_out[...] = (vec_z[0] + vec_z[1]) + (vec_z[2] + vec_z[3])

        def finish(j, carry):
            wait(reduce(j).finish)
            return carry

        lax.fori_loop(0, blocks, finish, 0)
        wait(tok_reduce.finish)

    inputs = dict(counts=(counts, SMEM), patches=(patches, ANYWHERE), grad_out=(grad_out, ANYWHERE))
    inputs.update({"p_" + name: (of, ANYWHERE if name[:6] == "w_chan" else VMEM) for name, of in params.items()})
    outputs = {name: (of, ANYWHERE) for name, of in layer_results(sz).items()}
    outputs.update(
        gathered=(((2, 4, 4, part, sz.hidden), BF16), ANYWHERE), own_out=(((2, part, sz.hidden), F32), VMEM),
        tok_fin=(((2, pack_rows, sz.lanes), F32), VMEM), vec_out=(((16, sz.channels), F32), VMEM),
    )
    scratch = layer_scratch(sz, (4, 4, part))
    for group in (layer_sums(sz), layer_params(sz)):
        scratch.update({name: pltpu.VMEM(*of) for name, of in group.items()})
    scratch.update({"c%d" % k: of for k, of in enumerate(reduce_scratch(part, width, 2))})
    scratch.update({"t%d" % k: of for k, of in enumerate(small_reduce_scratch(pack_rows, sz.lanes))})
    dma = pltpu.SemaphoreType.DMA
    scratch.update(
        pack_all=pltpu.VMEM((2, 4, 4, pack_rows, sz.lanes), BF16), pack_own=pltpu.VMEM((pack_rows, sz.lanes), BF16),
        pack_tmp=pltpu.VMEM((pack_rows, sz.lanes), F32), own_weight=pltpu.VMEM((part, sz.hidden), BF16),
        tok_out_bias=pltpu.VMEM((sz.padded, 1), F32),
        vec=pltpu.VMEM((16, sz.channels), F32), vec_in=pltpu.VMEM((16, sz.channels), F32),
        vec_xy=pltpu.VMEM((4, 16, sz.channels), F32), vec_z=pltpu.VMEM((4, 16, sz.channels), F32), own_sem=dma((3,)),
        gather_send=dma((n_gather * 7,)), gather_recv=dma((n_gather * 7,)),
        reduce_send=dma((n_reduce * 7,)), reduce_recv=dma((n_reduce * 7,)),
        tok_send=dma((8,)), tok_recv=dma((8,)), vector_send=dma((7,)), vector_recv=dma((7,)),
    )
    return call_kernel(kernel, inputs, outputs, scratch, 62, collective_id=0, has_side_effects=True)


def make_pack(sz, c, refs):
    tmp = refs.pack_tmp
    tok_in, tok_out = refs.p_w_token_in, refs.p_w_token_out
    tok_part = tok_out.shape[0]

    def row(*sources):
        values = [source[...].astype(F32)[None, :] for source in sources]
        rest = sz.lanes - sum(value.shape[1] for value in values)
        return jnp.concatenate(values + [jnp.zeros((1, rest), F32)], axis=1)

    tmp[...] = jnp.zeros_like(tmp)
    tmp[0:tok_part, 0 : sz.patches] = jnp.where(c == 0, tok_in[...].astype(F32), tok_out[...].astype(F32))
    first = row(refs.p_ln1_gain, refs.p_ln1_bias, refs.p_ln2_gain, refs.p_ln2_bias, refs.p_b_chan_out)
    tmp[tok_part : tok_part + 1, :] = jnp.where(c == 0, first, row(refs.p_b_chan_in, refs.p_b_token_in))
    refs.pack_own[...] = tmp[...].astype(BF16)
    bias = jnp.broadcast_to(row(refs.p_b_token_out), (8, sz.lanes))
    refs.tok_out_bias[...] = jnp.transpose(bias)[0 : sz.padded, 0:1]


def spread(rows, length, lanes, first_lane, columns):
    at = lax.broadcasted_iota(jnp.int32, (1, columns[1] - columns[0]), 1) + columns[0]
    device = jnp.zeros_like(at)
    for k in range(1, 16):
        device += jnp.where(at >= k * length, 1, 0)
    source = at - device * length + first_lane
    lane = lax.broadcasted_iota(jnp.int32, (lanes, source.shape[1]), 0)
    chosen = jnp.where(lane == source, 1.0, 0.0).astype(BF16)
    value = dot(rows, chosen, NN)
    owner = lax.broadcasted_iota(jnp.int32, value.shape, 0)
    return jnp.sum(jnp.where(owner == device, value, 0.0), axis=0, keepdims=True)


def unpack(sz, layer, pack_all, tok_part):
    pad, lanes, ch = sz.padded, sz.lanes, sz.channels
    rows = pack_all.shape[3]
    both = [pack_all[m].reshape(16, rows, lanes).astype(F32) for m in range(2)]
    first, second = (value[:, :tok_part].reshape(sz.token_hidden, lanes) for value in both)
    vectors, biases = (value[:, tok_part].astype(BF16) for value in both)
    part = ch // 16
    for v, ref in enumerate((layer.gain1, layer.shift1, layer.gain2, layer.shift2, layer.out_bias)):
        ref[...] = spread(vectors, part, lanes, v * part, (0, ch))
    for j in range(sz.blocks):
        layer.chan_in_bias[j] = spread(biases, sz.hidden // 16, lanes, 0, (j * sz.width, (j + 1) * sz.width))
    bias = spread(biases, tok_part, lanes, sz.hidden // 16, (0, sz.token_hidden))
    bias = jnp.transpose(jnp.broadcast_to(bias, (8, sz.token_hidden)))[:, 0:1]
    column = lax.broadcasted_iota(jnp.int32, first.shape, 1)
    layer.tok_in_t[...] = jnp.where(column == sz.patches, bias, first)[:, :pad].astype(BF16)
    layer.tok_out[...] = second[:, :pad].astype(BF16)
    layer.tok_in[...] = jnp.transpose(first)[:pad].astype(BF16)
    layer.tok_out_t[...] = jnp.transpose(second)[:pad].astype(BF16)


def hand_out(sz, raw, tok_part, hidden_part):
    part = raw.own_out.shape[1]
    images, patch, ch = sz.images, sz.patches, sz.channels

    def kernel(refs):
        load_sem, store_sem, own_sem = refs.load_sem, refs.store_sem, refs.own_sem

        def loads(i):
            return [
                pltpu.make_async_copy(refs.raw_mixed.at[i], refs.tmp_mixed.at[i], load_sem.at[0, i]),
                pltpu.make_async_copy(refs.raw_grad.at[i], refs.tmp_grad.at[i], load_sem.at[1, i]),
            ]

        def stores(i):
            return [
                pltpu.make_async_copy(refs.tmp_mixed.at[i], refs.mixed.at[i], store_sem.at[0, i]),
                pltpu.make_async_copy(refs.tmp_wide.at[i], refs.grad_patches.at[i], store_sem.at[1, i]),
            ]

        def load(i, carry):
            start(loads(i))
            return carry

        def store(i, carry):
            wait(loads(i))
            refs.tmp_wide[i] = refs.tmp_grad[i].astype(F32)
            start(stores(i))
            return carry

        def finish(i, carry):
            wait(stores(i))
            return carry

        own_loads = [pltpu.make_async_copy(refs.own, refs.tmp_own, own_sem.at[0])]
        own_stores = [
            pltpu.make_async_copy(refs.tmp_own.at[m], target, own_sem.at[1 + m])
            for m, target in enumerate((refs.g_chan_in, refs.g_chan_out))
        ]
        lax.fori_loop(0, images, load, 0)
        start(own_loads)
        lax.fori_loop(0, images, store, 0)
        wait(own_loads)
        start(own_stores)
        me = lax.axis_index("dp")
        vec, tok = refs.vec, refs.tok
        across = pltpu.roll(vec[...], ch - me * part, axis=1)
        for k, ref in enumerate((refs.g_gain1, refs.g_shift1, refs.g_gain2, refs.g_shift2, refs.g_out_bias)):
            ref[...] = across[k, 0:part]
        refs.g_tok_out_bias[...] = vec[5, 0:patch]
        per_row = ch // hidden_part
        row = vec[pl.ds(6 + me // per_row, 1), :]
        refs.g_chan_in_bias[...] = pltpu.roll(row, ch - lax.rem(me, per_row) * hidden_part, axis=1)[0, 0:hidden_part]
        refs.g_tok_out[...] = tok[1, 0:tok_part, 0:patch]
        refs.g_tok_in[...] = tok[0, 0:tok_part, 0:patch]
        refs.g_tok_in_bias[...] = jnp.transpose(tok[0])[patch, 0:tok_part]
        wait(own_stores)
        lax.fori_loop(0, images, finish, 0)

    inputs = dict(
        raw_mixed=(raw.mixed, ANYWHERE), raw_grad=(raw.grad_patches, ANYWHERE), own=(raw.own_out, ANYWHERE),
        tok=(raw.tok_fin, VMEM), vec=(raw.vec_out, VMEM),
    )
    vector, big = ((part,), F32), ((part, sz.hidden), F32)
    outputs = dict(
        mixed=(((images, patch, ch), BF16), ANYWHERE), grad_patches=(((images, patch, ch), F32), ANYWHERE),
        g_gain1=(vector, VMEM), g_shift1=(vector, VMEM), g_tok_in=(((tok_part, patch), F32), VMEM),
        g_tok_in_bias=(((tok_part,), F32), VMEM), g_tok_out=(((tok_part, patch), F32), VMEM),
        g_tok_out_bias=(((patch,), F32), VMEM), g_gain2=(vector, VMEM), g_shift2=(vector, VMEM),
        g_chan_in=(big, ANYWHERE), g_chan_in_bias=(((hidden_part,), F32), VMEM), g_chan_out=(big, ANYWHERE),
        g_out_bias=(vector, VMEM),
    )
    dma = pltpu.SemaphoreType.DMA
    scratch = dict(
        tmp_mixed=pltpu.VMEM((images, patch, ch), BF16), tmp_grad=pltpu.VMEM((images, patch, ch), BF16),
        tmp_wide=pltpu.VMEM((images, patch, ch), F32), tmp_own=pltpu.VMEM((2, part, sz.hidden), F32),
        load_sem=dma((2, images)), store_sem=dma((2, images)), own_sem=dma((3,)),
    )
    results = call_kernel(kernel, inputs, outputs, scratch, 62)
    results.g_tok_in, results.g_chan_out = results.g_tok_in.T, results.g_chan_out.T
    return tuple(vars(results).values())


def local(sz, counts, patches, grad_out, weights, tok_out_bias, params):
    def kernel(refs):
        layer = Layer(sz, refs)
        gw_slot, gw_sem = refs.gw_slot, refs.gw_sem

        def columns(j):
            return pl.ds(pl.multiple_of(j * sz.width, sz.width), sz.width)

        def weight_loads(j, slot):
            return [
                pltpu.make_async_copy(refs.weights.at[m, :, columns(j)], layer.w_slot.at[slot, m], layer.w_sem.at[slot, m])
                for m in range(2)
            ]

        def grad_stores(j, m):
            return [pltpu.make_async_copy(gw_slot.at[m], refs.g_weights.at[m, :, columns(j)], gw_sem.at[m])]

        layer.begin()
        start(weight_loads(0, 0))
        layer.clear()
        lax.fori_loop(0, sz.pairs, layer.mask_pair, 0)
        lax.fori_loop(0, sz.pairs, layer.norm_pair, 0)

        def forward_step(pair, carry):
            layer.token_forward(pair)
            return carry

        lax.fori_loop(0, sz.pairs, forward_step, 0)
        layer.token_forward_end()

        start(layer.back_copies(0, 0))

        def block_step(late, j, carry):
            slot = lax.rem(j, 2)
            wait(weight_loads(j, slot))

            @pl.when(j + 1 < sz.blocks)
            def _():
                start(weight_loads(j + 1, 1 - slot))

            def chunk(r, carry):
                layer.row_chunk(j, slot, r, late)
                return carry

            lax.fori_loop(0, sz.chunks, chunk, 0)
            for m in range(2):

                @pl.when(j >= 1)
                def _():
                    wait(grad_stores(j - 1, m))

                gw_slot[m] = layer.weight_grad(m, slot)
                start(grad_stores(j, m))
            return carry

        lax.fori_loop(0, sz.blocks - 2, functools.partial(block_step, False), 0)
        lax.fori_loop(sz.blocks - 2, sz.blocks, functools.partial(block_step, True), 0)
        for m in range(2):
            wait(grad_stores(sz.blocks - 1, m))

        def backward_step(pair, carry):
            layer.token_backward(pair)
            return carry

        lax.fori_loop(0, sz.pairs, backward_step, 0)
        layer.token_backward_end()

        def output(pair, carry):
            layer.finish_output(pair)
            return carry

        lax.fori_loop(0, sz.pairs, output, 0)
        layer.finish_output_end()

    inputs = dict(
        counts=(counts, SMEM), patches=(patches, ANYWHERE), grad_out=(grad_out, ANYWHERE), weights=(weights, ANYWHERE),
        tok_out_bias=(tok_out_bias, VMEM),
    )
    inputs.update({name: (params[name], VMEM) for name in layer_params(sz)})
    outputs = {name: (of, ANYWHERE) for name, of in layer_results(sz).items()}
    outputs.update(g_weights=(((2, sz.channels, sz.hidden), F32), ANYWHERE))
    outputs.update({name: (of, VMEM) for name, of in layer_sums(sz).items()})
    scratch = layer_scratch(sz, (sz.channels,))
    scratch.update(gw_slot=pltpu.VMEM((2, sz.channels, sz.width), F32), gw_sem=pltpu.SemaphoreType.DMA((2,)))
    return call_kernel(kernel, inputs, outputs, scratch, 62)


def on_device(
    patches, image_counts, grad_out,
    ln1_gain, ln1_bias, w_token_in, b_token_in, w_token_out, b_token_out,
    ln2_gain, ln2_bias, w_chan_in, b_chan_in, w_chan_out, b_chan_out,
):
    images, patch, ch = patches.shape
    token_part, hidden_part, part = b_token_in.shape[0], b_chan_in.shape[0], ln1_gain.shape[0]
    n_dp = lax.axis_size("dp")
    hidden = w_chan_in.shape[1]
    sz = Sizes(images, patch, ch, token_part * n_dp, hidden, 512, images * (-(-patch // 8) * 8) // 3)
    pad = sz.padded
    vectors = (ln1_gain, ln1_bias, ln2_gain, ln2_bias, b_chan_out)

    def own(vector, length):
        return lax.dynamic_slice_in_dim(vector, lax.axis_index("dp") * length, length)

    if n_dp == 16 and sz.pairs == 6 and part % 16 == 0 and token_part % 8 == 0 and part % token_part == 0:
        res = networked(
            sz, image_counts, patches, grad_out, ln1_gain=ln1_gain, ln1_bias=ln1_bias, w_token_in=w_token_in.T,
            b_token_in=b_token_in, w_token_out=w_token_out, b_token_out=b_token_out, ln2_gain=ln2_gain,
            ln2_bias=ln2_bias, w_chan_in=w_chan_in, b_chan_in=b_chan_in, w_chan_out=w_chan_out.T,
            b_chan_out=b_chan_out,
        )
        return hand_out(sz, res, token_part, hidden_part)
    else:
        tok_out_bias = jnp.pad(b_token_out.astype(F32), (0, pad - patch))[:, None]
        weights = lax.all_gather(jnp.stack([w_chan_in, w_chan_out.T]), "dp", axis=1, tiled=True)
        tokens = lax.all_gather(jnp.stack([w_token_in.T, w_token_out]), "dp", axis=1, tiled=True)
        tokens = jnp.pad(tokens, ((0, 0), (0, 0), (0, pad - patch)))
        every = lax.all_gather(jnp.concatenate(vectors + (b_token_in, b_chan_in)), "dp", axis=0)
        whole = [every[:, k * part : (k + 1) * part].reshape(1, ch).astype(F32) for k in range(5)]
        tok_bias = every[:, 5 * part : 5 * part + token_part].reshape(-1)
        gain1, shift1, gain2, shift2, out_bias = whole
        params = dict(
            gain1=gain1, shift1=shift1, gain2=gain2, shift2=shift2, out_bias=out_bias,
            tok_in_t=tokens[0].at[:, patch].set(tok_bias), tok_in=tokens[0].T,
            tok_out_t=tokens[1].T, tok_out=tokens[1],
            chan_in_bias=every[:, 5 * part + token_part :].reshape(sz.blocks, 1, sz.width).astype(F32),
        )
        res = local(sz, image_counts, patches, grad_out, weights, tok_out_bias, params)
        g_weights = lax.psum_scatter(res.g_weights.astype(BF16), "dp", scatter_dimension=1, tiled=True)
        g_weights = lax.psum(g_weights, "outer").astype(F32)
        g_tokens = lax.psum(lax.psum_scatter(res.g_tok, "dp", scatter_dimension=1, tiled=True), "outer")
        sums = [jnp.sum(v, axis=0) for v in (res.g_gain1, res.g_shift1, res.g_gain2, res.g_shift2, res.g_out_bias)]
        sums += [jnp.sum(res.g_chan_in_bias, axis=1).reshape(-1), res.g_tok_out_bias[:patch, 0]]
        sums = lax.psum(tuple(sums), ("dp", "outer"))
        g_vec = [own(vector, part) for vector in sums[:5]]
        g_chan_bias, g_tok_out_bias = own(sums[5], hidden_part), sums[6]

    return (
        res.mixed, res.grad_patches.astype(F32),
        g_vec[0], g_vec[1], g_tokens[0, :, :patch].T, g_tokens[0, :, patch], g_tokens[1, :, :patch], g_tok_out_bias,
        g_vec[2], g_vec[3], g_weights[0], g_chan_bias, g_weights[1].T, g_vec[4],
    )


def solution(mesh):
    slots = P(("dp", "outer"), None, None)
    return jax.shard_map(
        on_device,
        mesh=mesh,
        in_specs=(
            slots, P(("dp", "outer")), slots, P("dp"), P("dp"), P(None, "dp"), P("dp"), P("dp", None), P(),
            P("dp"), P("dp"), P("dp", None), P("dp"), P(None, "dp"), P("dp"),
        ),
        out_specs=(
            slots, slots, P("dp"), P("dp"), P(None, "dp"), P("dp"), P("dp", None), P(),
            P("dp"), P("dp"), P("dp", None), P("dp"), P(None, "dp"), P("dp"),
        ),
        check_vma=False,
    )
```
